128 devices in a mesh: ctx: 8 (over z_lo, x), tp: 16 (over y, z_hi, core).
Axes of the slice: x: 4, y: 4, z: 4 (z_hi: 2, z_lo: 2; z = z_hi * 2 + z_lo), core: 2. Of those that a mesh axis runs over, the one named last changes fastest.
Arguments:
- tokens: bfloat16 [8192, 4096], P('ctx', 'tp'), may hold values from -6 to 6
- norm_gain: float32 [4096], replicated, may hold values from 0.1 to 1.9
- w_in: bfloat16 [4096, 3, 4096], P(None, None, 'tp'), may hold values from -0.09375 to 0.09375
- w_short: float32 [7, 3, 4096], P(None, None, 'tp'), may hold values from -2 to 2
- decay_rate: float32 [4096, 16], P('tp'), may hold values from 5e-05 to 0.05
- residue: float32 [4096, 16], P('tp'), may hold values from -1.5 to 1.5
- w_out: bfloat16 [4096, 4096], P(None, 'tp'), may hold values from -0.09375 to 0.09375
Outputs:
- output: bfloat16 [8192, 4096], P('ctx', 'tp')
The draws below stay inside these ranges and needn't reach their ends.
All inputs are finite; a program needn't handle non-finite values.
Results may differ from the reference program's by a relative error of at most 0.015.
Values may be sent and summed in bfloat16 or wider, within the bound.
No kernel may reach another device: no remote copies, remote signals or barrier semaphores. Data moves between devices by JAX's collectives and lax.ppermute only.
A program may use at most 128 MiB of HBM per device.

```python
import math
import jax
import jax.numpy as jnp
from jax import lax

D = 4096
ORDER = 16
SHORT = 7
SEQ = 8192


def shard_levels(key, shape, pieces, least, largest):
    def one(position, parts):
        steps = jax.random.uniform(jax.random.fold_in(jax.random.fold_in(key, 6), position), (parts,), jnp.float32, least / len(pieces), largest / len(pieces))
        return jnp.repeat(jnp.exp(steps), shape[position] // parts).reshape((-1,) + (1,) * (len(shape) - position - 1))

    gain = one(*pieces[0])
    for cut in pieces[1:]:
        gain = gain * one(*cut)
    return gain


def bell_draw(own_key, extent, spread, most, split=(), dtype=jnp.bfloat16):
    drawn = spread * jax.random.normal(own_key, extent, jnp.float32)
    if split:
        drawn = drawn * shard_levels(own_key, extent, split, -0.22, 0.18)
    return jnp.clip(drawn, -most, most).astype(dtype)


def setup_inputs(seed: int = 0) -> dict:
    key_list = jax.random.split(jax.random.key(seed), 8)
    tokens = bell_draw(key_list[0], (SEQ, D), 1.0, 6.0, ((0, 8), (1, 16)))
    norm_gain = jnp.clip(1.0 + 0.18 * jax.random.normal(key_list[1], (D,), jnp.float32), 0.1, 1.9)
    w_in = bell_draw(key_list[2], (D, 3, D), D ** -0.5, 0.09375, ((2, 16),))
    w_short = bell_draw(key_list[3], (SHORT, 3, D), SHORT ** -0.5, 2.0, ((2, 16),), jnp.float32)
    decay_rate = jnp.clip(jnp.exp(math.log(0.05) - 6.9077553 * jax.random.uniform(key_list[4], (D, ORDER), jnp.float32) ** shard_levels(key_list[4], (D, ORDER), ((0, 16),), -0.2, 0.2)), 4.999999873689376e-05, 0.05)
    residue = bell_draw(key_list[5], (D, ORDER), ORDER ** -0.5, 1.5, ((0, 16),), jnp.float32)
    w_out = bell_draw(key_list[6], (D, D), D ** -0.5, 0.09375, ((1, 16),))
    return dict(tokens=tokens, norm_gain=norm_gain, w_in=w_in, w_short=w_short, decay_rate=decay_rate, residue=residue, w_out=w_out)


def filter_block(args):
    kv_rows, rate, residue = args
    lags = jnp.arange(SEQ).astype(jnp.float32)
    weight_res = residue * jnp.sqrt(rate)
    decay = jnp.exp(-rate[:, :, None] * lags[None, None, :])
    filt = jnp.einsum('cn,cnt->ct', weight_res, decay, precision=lax.Precision.HIGHEST)
    size = 2 * SEQ
    spectrum = jnp.fft.rfft(kv_rows, n=size, axis=1) * jnp.fft.rfft(filt, n=size, axis=1)
    return jnp.fft.irfft(spectrum, n=size, axis=1)[:, :SEQ]

def reference(tokens, norm_gain, w_in, w_short, decay_rate, residue, w_out):
    wide = tokens.astype(jnp.float32)
    scale = lax.rsqrt(lax.optimization_barrier(jnp.mean(wide * wide, axis=1, keepdims=True)) + 1e-05)
    normed = (wide * scale * norm_gain).astype(jnp.bfloat16)
    proj = jnp.dot(normed, w_in.reshape(D, 3 * D), preferred_element_type=jnp.float32)
    proj = proj.astype(jnp.bfloat16).reshape(SEQ, 3, D)
    padded = jnp.pad(proj.astype(jnp.float32), ((SHORT - 1, 0), (0, 0), (0, 0)))
    short = jnp.zeros((SEQ, 3, D), jnp.float32)
    for offset in range(SHORT):
        begin = SHORT - 1 - offset
        short = short + w_short[offset] * padded[begin:begin + SEQ]
    gate_q = short[:, 0].astype(jnp.bfloat16)
    gated_kv = (short[:, 1] * short[:, 2]).astype(jnp.bfloat16)
    width = min(D, 128)
    kv_rows = gated_kv.astype(jnp.float32).T.reshape(D // width, width, SEQ)
    long_rows = lax.map(filter_block, (kv_rows, decay_rate.reshape(D // width, width, ORDER), residue.reshape(D // width, width, ORDER)))
    long_out = long_rows.reshape(D, SEQ).T
    mixed = (gate_q.astype(jnp.float32) * long_out).astype(jnp.bfloat16)
    result = jnp.dot(mixed, w_out, preferred_element_type=jnp.float32) + wide
    return result.astype(jnp.bfloat16)
```

```python
import jax
import jax.numpy as jnp
from jax import lax
from jax.experimental import pallas as pl
from jax.experimental.pallas import tpu as pltpu
from jax.sharding import PartitionSpec as P

F32 = jnp.float32
BF16 = jnp.bfloat16
MODES = 16
SPAN = 7
REACH = SPAN - 1
LANES = 128
SUBS = 8
VMEM = pl.BlockSpec(memory_space=pltpu.VMEM)
HBM = pl.BlockSpec(memory_space=pl.ANY)
SMEM = pl.BlockSpec(memory_space=pltpu.SMEM)
MIB = 1024 * 1024


def call(kernel, outs, ins, specs, scratch, limit, flops, aliases=None):
    moved = sum(a.size * a.dtype.itemsize for a in ins)
    return pl.pallas_call(
        kernel,
        out_shape=outs,
        in_specs=specs,
        out_specs=[VMEM] * len(outs) if isinstance(outs, list) else VMEM,
        scratch_shapes=scratch,
        input_output_aliases=aliases or {},
        compiler_params=pltpu.CompilerParams(vmem_limit_bytes=limit * MIB),
        cost_estimate=pl.CostEstimate(flops=flops, bytes_accessed=moved // 4, transcendentals=0),
    )(*ins)


def order_kernel(order, w_in, w_out, first, second, sems):
    count = first.shape[0]
    width = first.shape[2]
    copies = []
    for i in range(count):
        rows = pl.ds(pl.multiple_of(order[i] * width, width), width)
        copies.append(pltpu.make_async_copy(w_in.at[:, rows, :], first.at[i], sems.at[0, i]))
        copies.append(pltpu.make_async_copy(w_out.at[rows, :], second.at[i], sems.at[1, i]))
    for copy in copies:
        copy.start()
    for copy in copies:
        copy.wait()


def add_pieces(begin, layout, order, gain, w, refs, r, tile):
    total = [None] * 3
    squares = None
    for number, parts in enumerate(layout):
        x = refs_rows(refs, parts, r, tile).astype(F32)
        row = gain[pl.ds(order[begin + number], 1), :]
        scaled = (x * row).astype(BF16)
        square = x * x
        square = square[:, :LANES] + square[:, LANES:]
        squares = square if squares is None else squares + square
        for s in range(3):
            part = jnp.dot(scaled, w[begin + number, s], preferred_element_type=F32)
            total[s] = part if total[s] is None else total[s] + part
    return total, squares


def refs_rows(refs, parts, r, tile):
    if len(parts) == 1:
        return refs[parts[0]][pl.ds(r * tile, tile), :]
    half = refs[parts[0]].shape[0]
    if r * tile < half:
        return refs[parts[0]][pl.ds(r * tile, tile), :]
    return refs[parts[1]][pl.ds(r * tile - half, tile), :]


def proj_kernel(begin, layout, fresh, order, gain, w, *refs):
    count = sum(len(p) for p in layout)
    pieces = refs[:count]
    if fresh:
        acc, ss = refs[count:]
    else:
        acc_in, ss_in, acc, ss = refs[count:]
    tile = 256
    for r in range(acc.shape[0] // tile):
        rows = pl.ds(r * tile, tile)
        total, squares = add_pieces(begin, layout, order, gain, w, pieces, r, tile)
        for s in range(3):
            cols = slice(s * 256, (s + 1) * 256)
            acc[rows, cols] = total[s] if fresh else acc_in[rows, cols] + total[s]
        ss[rows, :] = squares if fresh else ss_in[rows, :] + squares


def number(pieces):
    layout, flat = [], []
    for p in pieces:
        parts = p if isinstance(p, tuple) else (p,)
        layout.append(tuple(range(len(flat), len(flat) + len(parts))))
        flat.extend(parts)
    return layout, flat


def project(begin, pieces, order, gain, w, state):
    layout, flat = number(pieces)
    rows = flat[0].shape[0] * len(layout[0])
    outs = [jax.ShapeDtypeStruct((rows, 768), F32), jax.ShapeDtypeStruct((rows, LANES), F32)]
    ins = [order, gain, w] + flat + (list(state) if state else [])
    specs = [SMEM, VMEM, VMEM] + [VMEM] * (len(ins) - 3)
    fresh = state is None

    def kernel(*refs):
        proj_kernel(begin, layout, fresh, *refs)

    aliases = {} if fresh else {len(ins) - 2: 0, len(ins) - 1: 1}
    return call(kernel, outs, ins, specs, [], 16, len(pieces) * 2 * rows * 256 * 768, aliases)


def local_kernel(begin, layout, chunk, order, gain, w, *refs):
    count = sum(len(p) for p in layout)
    pieces = refs[:count]
    acc, ss, taps, decay, weight, jumps, gate, local, before, load, proj = refs[count:]
    tile = 256
    width = gate.shape[1]
    rows_all = acc.shape[0]
    halves = width // LANES
    proj[:, 0:8, :] = jnp.zeros((3 * halves, 8, LANES), F32)
    for r in range(rows_all // tile):
        rows = pl.ds(r * tile, tile)
        total, squares = add_pieces(begin, layout, order, gain, w, pieces, r, tile)
        mean = jnp.sum(ss[rows, :] + squares, axis=1, keepdims=True) / (16 * width)
        scale = lax.rsqrt(mean + 1e-05)
        for s in range(3):
            cols = slice(s * 256, (s + 1) * 256)
            value = (acc[rows, cols] + total[s]) * scale
            value = value.astype(BF16).astype(F32)
            for g in range(halves):
                proj[s * halves + g, pl.ds(8 + r * tile, tile), :] = value[:, g * LANES : (g + 1) * LANES]
    head = lax.broadcasted_iota(jnp.int32, (SUBS, LANES), 0) == 0
    for g in range(width // LANES):
        lanes = slice(g * LANES, (g + 1) * LANES)

        def strided(s, t):
            return proj[s * halves + g, pl.ds(8 + t, SUBS, stride=chunk), :]

        def step(t, carry, masked):
            windows, states = carry
            short = []
            moved = []
            for s in range(3):
                newest = strided(s, t)
                line = windows[s] + [newest]
                value = None
                for j in range(SPAN):
                    at = (j * 3 + s) * SUBS
                    term = taps[at : at + SUBS, lanes] * line[REACH - j]
                    value = term if value is None else value + term
                short.append(value)
                moved.append(line[1:])
            kv = (short[1] * short[2]).astype(BF16).astype(F32)
            if masked:
                kv = jnp.where(head, 0.0, kv)
            out = None
            later = []
            for n in range(MODES):
                at = n * SUBS
                state = decay[at : at + SUBS, lanes] * states[n] + kv
                later.append(state)
                term = weight[at : at + SUBS, lanes] * state
                out = term if out is None else out + term
            place = pl.ds(pl.multiple_of(t * SUBS, SUBS), SUBS)
            gate[place, lanes] = short[0].astype(BF16).astype(F32)
            local[place, lanes] = out
            return moved, later

        windows = [
            [strided(s, t) for t in range(-REACH, 0)]
            for s in range(3)
        ]
        carry = (windows, [jnp.zeros((SUBS, LANES), F32)] * MODES)
        unroll = 8
        for t in range(unroll):
            carry = step(t, carry, t < REACH)

        def steps(i, carry):
            for u in range(unroll):
                carry = step(i * unroll + u, carry, False)
            return carry

        carry = lax.fori_loop(1, chunk // unroll, steps, carry)
        place = lax.broadcasted_iota(jnp.int32, (SUBS, LANES), 0)
        for n in range(MODES):
            at = n * SUBS
            state = carry[1][n]
            for level, hop in enumerate((1, 2, 4)):
                moved = jnp.where(place >= hop, pltpu.roll(state, hop, 0), 0.0)
                jump = jumps[level * MODES + n : level * MODES + n + 1, lanes]
                state = state + jump * moved
            before[at : at + SUBS, lanes] = jnp.where(place >= 1, pltpu.roll(state, 1, 0), 0.0)
            load[n : n + 1, lanes] = state[SUBS - 1 : SUBS, :]
    for s in range(3):
        for g in range(halves):
            lanes = slice(g * LANES, (g + 1) * LANES)
            load[16 + s * 16 : 24 + s * 16, lanes] = proj[s * halves + g, rows_all : rows_all + 8, :]
            load[24 + s * 16 : 32 + s * 16, lanes] = proj[s * halves + g, 8:16, :]


def join_kernel(chunk, *refs):
    loads = refs[:8]
    gate, local, before, taps, decay, weight, power, power_less, ahead, early, late = refs[8:19]
    mixed, held, whole, start = refs[19:]
    step_rows = loads[0].shape[0]
    width = mixed.shape[1]
    for g in range(width // LANES):
        for d in range(8):
            held[g, d * step_rows : (d + 1) * step_rows, :] = loads[d][:, g * LANES : (g + 1) * LANES]
        held[g, 8 * step_rows : 9 * step_rows, :] = jnp.zeros((step_rows, LANES), F32)
    place = lax.broadcasted_iota(jnp.int32, (SUBS, LANES), 0)
    head = place == 0
    for g in range(width // LANES):
        lanes = slice(g * LANES, (g + 1) * LANES)

        def strided(row):
            return held[g, pl.ds(row, SUBS, stride=step_rows), :]

        short = []
        for s in range(3):
            line = [strided(step_rows + 16 + s * 16 + 8 - REACH + t) for t in range(REACH)]
            line += [strided(24 + s * 16 + t) for t in range(REACH)]
            values = []
            for t in range(REACH):
                value = None
                for j in range(SPAN):
                    at = (j * 3 + s) * SUBS
                    term = taps[at : at + SUBS, lanes] * line[REACH + t - j]
                    value = term if value is None else value + term
                values.append(value)
            short.append(values)
        kv = [(short[1][t] * short[2][t]).astype(BF16).astype(F32) for t in range(REACH)]
        q = [short[0][t].astype(BF16).astype(F32) for t in range(REACH)]
        for n in range(MODES):
            at = n * SUBS
            full = strided(n)
            own = None
            for t in range(REACH):
                row = t * MODES + n
                full = full + late[row : row + 1, lanes] * kv[t]
                term = early[row : row + 1, lanes] * kv[t]
                own = term if own is None else own + term
            arrived = jnp.sum(ahead[at : at + SUBS, lanes] * full, axis=0, keepdims=True)
            state = before[at : at + SUBS, lanes] + power[at : at + SUBS, lanes] * arrived
            state = state + power_less[at : at + SUBS, lanes] * own[0:1, :]
            start[at : at + SUBS, lanes] = state * weight[at : at + SUBS, lanes]

        def step(t, states, extra, fixed):
            out = None
            later = []
            for n in range(MODES):
                at = n * SUBS
                state = decay[at : at + SUBS, lanes] * states[n]
                if extra is not None:
                    state = state + weight[at : at + SUBS, lanes] * extra
                later.append(state)
                out = state if out is None else out + state
            rows = pl.ds(pl.multiple_of(t * SUBS, SUBS), SUBS)
            q_now = gate[rows, lanes]
            if fixed is not None:
                q_now = jnp.where(head, fixed, q_now)
            whole[g, pl.ds(t, SUBS, stride=chunk), :] = q_now * (out + local[rows, lanes])
            return later

        states = [start[n * SUBS : (n + 1) * SUBS, lanes] for n in range(MODES)]
        unroll = 8
        for t in range(unroll):
            first = t < REACH
            extra = jnp.where(head, kv[t], 0.0) if first else None
            states = step(t, states, extra, q[t] if first else None)

        def steps(i, states):
            for u in range(unroll):
                states = step(i * unroll + u, states, None, None)
            return states

        lax.fori_loop(1, chunk // unroll, steps, states)
    for g in range(width // LANES):
        mixed[:, g * LANES : (g + 1) * LANES] = whole[g].astype(BF16)


def out_kernel(begin, layout, fresh, last, w, *refs):
    count = sum(len(p) for p in layout)
    pieces = refs[:count]
    rest = list(refs[count:])
    acc_in = None if fresh else rest.pop(0)
    tokens = rest.pop(0) if last else None
    out = rest.pop(0)
    tile = 256
    for r in range(out.shape[0] // tile):
        rows = pl.ds(r * tile, tile)
        total = None if fresh else acc_in[rows, :]
        for i, parts in enumerate(layout):
            x = refs_rows(pieces, parts, r, tile)
            part = jnp.dot(x, w[begin + i], preferred_element_type=F32)
            total = part if total is None else total + part
        if last:
            total = total + tokens[rows, :].astype(F32)
        out[rows, :] = total.astype(out.dtype)


def out_project(begin, pieces, w, state, tokens=None):
    layout, flat = number(pieces)
    rows = flat[0].shape[0] * len(layout[0])
    last = tokens is not None
    ins = [w] + flat + ([] if state is None else [state]) + ([tokens] if last else [])

    def kernel(*refs):
        out_kernel(begin, layout, state is None, last, *refs)

    outs = jax.ShapeDtypeStruct((rows, 256), BF16 if last else F32)
    aliases = {1 + len(flat): 0} if (state is not None and not last) else {}
    return call(
        kernel, outs, ins, [VMEM] * len(ins), [], 12, len(pieces) * 2 * rows * 256 * 256, aliases
    )


def shifted(x, dy, dz, dc):
    pairs = []
    for i in range(16):
        y, z, c = i // 4, (i // 2) % 2, i % 2
        pairs.append((i, ((y + dy) % 4) * 4 + ((z + dz) % 2) * 2 + (c + dc) % 2))
    return lax.ppermute(x, "tp", pairs)


def gather(x):
    half = x.shape[0] // 2
    other = lambda p: shifted(p, 0, 0, 1)
    left = shifted(x, 1, 0, 0)
    right = shifted(x, -1, 0, 0)
    up = shifted(x, 0, 1, 0)
    far = (shifted(left[:half], 1, 0, 0), shifted(right[half:], -1, 0, 0))
    up_left = shifted(up, 1, 0, 0)
    up_right = shifted(up, -1, 0, 0)
    up_far = tuple(shifted(p, 0, 1, 0) for p in far)
    groups = [[x], [left, right], [up], [far], [up_left, up_right], [up_far]]
    result = []
    for group in groups:
        pieces = []
        for p in group:
            pieces.append(p)
            pieces.append(tuple(other(h) for h in p) if isinstance(p, tuple) else other(p))
        result.append(pieces)
    return result


def body(tokens, norm_gain, w_in, w_short, decay_rate, residue, w_out):
    length, chans = tokens.shape
    chunk = length // SUBS
    me = lax.axis_index("tp")
    y, z, c = me // 4, (me // 2) % 2, me % 2
    places = [(0, 0), (-1, 0), (1, 0), (0, 1), (2, 0), (-1, 1), (1, 1), (2, 1)]
    order = jnp.stack(
        [
            ((y + dy) % 4) * 4 + ((z + dz) % 2) * 2 + (c + dc) % 2
            for dy, dz in places
            for dc in (0, 1)
        ]
    ).astype(jnp.int32)
    first, second = pl.pallas_call(
        order_kernel,
        out_shape=[
            jax.ShapeDtypeStruct((16, 3, chans, chans), BF16),
            jax.ShapeDtypeStruct((16, chans, chans), BF16),
        ],
        in_specs=[SMEM, HBM, HBM],
        out_specs=[VMEM, VMEM],
        scratch_shapes=[pltpu.SemaphoreType.DMA((2, 16))],
        compiler_params=pltpu.CompilerParams(vmem_limit_bytes=2 * MIB),
        cost_estimate=pl.CostEstimate(flops=0, bytes_accessed=8 * MIB, transcendentals=0),
    )(order, w_in.transpose(1, 0, 2), w_out)

    rate = decay_rate.T
    gain = norm_gain.reshape(16, chans)

    def rows8(table):
        return jnp.broadcast_to(table[:, None, :], (table.shape[0], SUBS, chans)).reshape(-1, chans)

    def powers(counts):
        counts = jnp.asarray(counts, F32)
        return jnp.exp(-rate[:, None, :] * counts[None, :, None])

    decay = rows8(jnp.exp(-rate))
    weight = rows8((residue * jnp.sqrt(decay_rate)).T)
    taps = rows8(w_short.reshape(SPAN * 3, chans))
    jumps = jnp.concatenate([jnp.exp(-rate * (chunk * hop)) for hop in (1, 2, 4)])
    power = powers([chunk * k for k in range(SUBS)])
    off = jnp.zeros((MODES, 1, chans), F32)
    power_less = jnp.concatenate([off, power[:, :-1]], axis=1).reshape(-1, chans)
    ahead = jnp.concatenate([off, powers([length * d for d in range(7)])], axis=1).reshape(-1, chans)
    power = power.reshape(-1, chans)
    early = jnp.concatenate([jnp.exp(-rate * (chunk - 1 - t)) for t in range(REACH)])
    late = jnp.concatenate([jnp.exp(-rate * (length - 1 - t)) for t in range(REACH)])

    groups = gather(tokens)
    state = None
    begin = 0
    for pieces in groups[:-1]:
        state = project(begin, pieces, order, gain, first, state)
        begin += len(pieces)
    layout, flat = number(groups[-1])
    ins = [order, gain, first] + flat + list(state) + [taps, decay, weight, jumps]

    def kernel(*refs):
        local_kernel(begin, layout, chunk, *refs)

    gate, local, before, load = call(
        kernel,
        [
            jax.ShapeDtypeStruct((length, chans), F32),
            jax.ShapeDtypeStruct((length, chans), F32),
            jax.ShapeDtypeStruct((MODES * SUBS, chans), F32),
            jax.ShapeDtypeStruct((64, chans), F32),
        ],
        ins,
        [SMEM] + [VMEM] * (len(ins) - 1),
        [pltpu.VMEM((3 * chans // LANES, length + 8, LANES), F32)],
        20,
        4 * 10**9,
    )
    loads = [load]
    for d in range(1, 8):
        loads.append(lax.ppermute(load, "ctx", [(i, i + d) for i in range(8 - d)]))
    ins = loads + [gate, local, before, taps, decay, weight, power, power_less, ahead, early, late]

    def kernel_two(*refs):
        join_kernel(chunk, *refs)

    mixed = call(
        kernel_two,
        jax.ShapeDtypeStruct((length, chans), BF16),
        ins,
        [VMEM] * len(ins),
        [
            pltpu.VMEM((chans // LANES, 9 * 64, LANES), F32),
            pltpu.VMEM((chans // LANES, length, LANES), F32),
            pltpu.VMEM((MODES * SUBS, chans), F32),
        ],
        12,
        2 * 10**9,
    )
    groups = gather(mixed)
    acc = None
    begin = 0
    for pieces in groups[:-1]:
        acc = out_project(begin, pieces, second, acc)
        begin += len(pieces)
    return out_project(begin, groups[-1], second, acc, tokens)


def solution(mesh):
    placed = (
        P("ctx", "tp"),
        P(),
        P(None, None, "tp"),
        P(None, None, "tp"),
        P("tp", None),
        P("tp", None),
        P(None, "tp"),
    )
    return jax.shard_map(
        body, mesh=mesh, in_specs=placed, out_specs=P("ctx", "tp"), check_vma=False
    )
```

```python
import jax
import jax.numpy as jnp
from jax import lax
from jax.experimental import pallas as pl
from jax.experimental.pallas import tpu as pltpu
from jax.sharding import PartitionSpec as P

F32 = jnp.float32
BF16 = jnp.bfloat16
MODES = 16
SPAN = 7
REACH = SPAN - 1
LANES = 128
SUBS = 8
VMEM = pl.BlockSpec(memory_space=pltpu.VMEM)
HBM = pl.BlockSpec(memory_space=pltpu.HBM)
SMEM = pl.BlockSpec(memory_space=pltpu.SMEM)
MIB = 1024 * 1024
TILE = 512


def call(kernel, outs, ins, specs, scratch, limit, flops, aliases=None):
    moved = sum(a.size * a.dtype.itemsize for a in ins)
    return pl.pallas_call(
        kernel,
        out_shape=outs,
        in_specs=specs,
        out_specs=[VMEM] * len(outs) if isinstance(outs, list) else VMEM,
        scratch_shapes=scratch,
        input_output_aliases=aliases or {},
        compiler_params=pltpu.CompilerParams(vmem_limit_bytes=limit * MIB),
        cost_estimate=pl.CostEstimate(flops=1, bytes_accessed=1, transcendentals=0),
    )(*ins)


TABLE = {}
for _name, _rows in (
    ("decay", MODES * SUBS),
    ("weight", MODES * SUBS),
    ("power", MODES * SUBS),
    ("power_less", MODES * SUBS),
    ("ahead", MODES * SUBS),
    ("taps", SPAN * 3 * SUBS),
    ("jumps", 3 * MODES),
    ("early", REACH * MODES),
    ("late", REACH * MODES),
):
    TABLE[_name] = (sum(rows for _, rows in TABLE.values()), _rows)
TABLE_ROWS = sum(rows for _, rows in TABLE.values())
PLACES = (
    ((0, 0, 0), (0, 0, 1), (0, 1, 0), (0, 1, 1), (2, 0, 0), (2, 0, 1), (2, 1, 0), (-1, 0, 0))
    + ((-1, 1, 0), (1, 0, 0), (1, 1, 0), (2, 1, 1), (-1, 0, 1), (-1, 1, 1), (1, 0, 1), (1, 1, 1))
)


def part(table, name):
    begin, rows = TABLE[name]
    return table.at[pl.ds(begin, rows)]


def order_kernel(chunk, w_in, w_out, gain, rate, residue, short, first, second, scale, table, sems):
    me = lax.axis_index("tp")
    y, z, c = me // 4, (me // 2) % 2, me % 2
    width = second.shape[1]
    copies = []
    for i in range(16):
        dy, dz, dc = PLACES[i]
        source = ((y + dy + 4) % 4) * 4 + ((z + dz) % 2) * 2 + (c + dc) % 2
        rows = pl.ds(pl.multiple_of(source * width, width), width)
        place = pl.ds(i * width, width)
        copies.append(pltpu.make_async_copy(w_in.at[:, rows, :], first.at[:, place, :], sems.at[0, i]))
        copies.append(pltpu.make_async_copy(w_out.at[rows, :], second.at[place, :], sems.at[1, i]))
        scale[i : i + 1, :] = gain[pl.ds(source, 1), :]
    for copy in copies:
        copy.start()

    length = SUBS * chunk
    sub = lax.broadcasted_iota(jnp.int32, (SUBS, width), 0)
    lag = sub.astype(F32)

    def put(name, row, value):
        at = TABLE[name][0] + row
        table[at : at + value.shape[0], :] = value

    rates = rate[...]
    for level, hop in enumerate((1, 2, 4)):
        put("jumps", level * MODES, jnp.exp(-rates * (chunk * hop)))
    for t in range(REACH):
        put("early", t * MODES, jnp.exp(-rates * (chunk - 1 - t)))
        put("late", t * MODES, jnp.exp(-rates * (length - 1 - t)))
    weights = residue[...] * jnp.sqrt(rates)
    decays = jnp.exp(-rates)
    for n in range(MODES):
        wide = jnp.broadcast_to(rates[n : n + 1, :], (SUBS, width))
        put("decay", n * SUBS, jnp.broadcast_to(decays[n : n + 1, :], (SUBS, width)))
        put("weight", n * SUBS, jnp.broadcast_to(weights[n : n + 1, :], (SUBS, width)))
        put("power", n * SUBS, jnp.exp(-wide * (lag * chunk)))
        less = jnp.exp(-wide * (jnp.maximum(lag - 1.0, 0.0) * chunk))
        put("power_less", n * SUBS, jnp.where(sub >= 1, less, 0.0))
        far = jnp.exp(-wide * (jnp.maximum(lag - 1.0, 0.0) * length))
        put("ahead", n * SUBS, jnp.where(sub >= 1, far, 0.0))
    for i in range(SPAN * 3):
        put("taps", i * SUBS, jnp.broadcast_to(short[i : i + 1, :], (SUBS, width)))
    for copy in copies:
        copy.wait()


def add_pieces(begin, layout, gain, w, refs, r, tile):
    squares = None
    scaled = []
    for number, piece in enumerate(layout):
        x = piece_rows(refs, piece, r, tile).astype(F32)
        scaled.append((x * gain[begin + number : begin + number + 1, :]).astype(BF16))
        square = x * x
        square = square[:, :LANES] + square[:, LANES:]
        squares = square if squares is None else squares + square
    scaled = jnp.concatenate(scaled, axis=1)
    rows = slice(begin * 256, (begin + len(layout)) * 256)
    total = [jnp.dot(scaled, w[s, rows, :], preferred_element_type=F32) for s in range(3)]
    return total, squares


def piece_rows(refs, piece, r, tile):
    number, first = piece
    return refs[number][pl.ds(first + r * tile, tile), :]


def proj_kernel(begin, layout, fresh, gain, w, *refs):
    count = 1 + max(p[0] for p in layout)
    pieces = refs[:count]
    if fresh:
        acc, ss = refs[count:]
    else:
        acc_in, ss_in, acc, ss = refs[count:]
    tile = TILE
    for r in range(acc.shape[0] // tile):
        rows = pl.ds(r * tile, tile)
        total, squares = add_pieces(begin, layout, gain, w, pieces, r, tile)
        for s in range(3):
            cols = slice(s * 256, (s + 1) * 256)
            acc[rows, cols] = total[s] if fresh else acc_in[rows, cols] + total[s]
        ss[rows, :] = squares if fresh else ss_in[rows, :] + squares


def number(pieces):
    layout, flat = [], []
    for piece in pieces:
        array, first = piece if isinstance(piece, tuple) else (piece, 0)
        known = [i for i, a in enumerate(flat) if a is array]
        if not known:
            flat.append(array)
        layout.append((known[0] if known else len(flat) - 1, first))
    return layout, flat


def project(length, begin, pieces, gain, w, state):
    layout, flat = number(pieces)
    rows = length
    outs = [jax.ShapeDtypeStruct((rows, 768), F32), jax.ShapeDtypeStruct((rows, LANES), F32)]
    ins = [gain, w] + flat + (list(state) if state else [])
    specs = [VMEM] * len(ins)
    fresh = state is None

    def kernel(*refs):
        proj_kernel(begin, layout, fresh, *refs)

    aliases = {} if fresh else {len(ins) - 2: 0, len(ins) - 1: 1}
    return call(kernel, outs, ins, specs, [], 16, len(pieces) * 2 * rows * 256 * 768, aliases)


def local_kernel(begin, layout, chunk, gain, w, *refs):
    count = 1 + max(p[0] for p in layout)
    pieces = refs[:count]
    acc, ss, table, gate, local, before, load, proj, last = refs[count:]
    taps, decay, weight, jumps = (part(table, n) for n in ("taps", "decay", "weight", "jumps"))
    tile = TILE
    width = gate.shape[1]
    rows_all = acc.shape[0]
    halves = width // LANES
    proj[:, 0:8, :] = jnp.zeros((3 * halves, 8, LANES), F32)
    for r in range(rows_all // tile):
        rows = pl.ds(r * tile, tile)
        total, squares = add_pieces(begin, layout, gain, w, pieces, r, tile)
        mean = jnp.sum(ss[rows, :] + squares, axis=1, keepdims=True) / (16 * width)
        scale = lax.rsqrt(mean + 1e-05)
        for s in range(3):
            cols = slice(s * 256, (s + 1) * 256)
            value = (acc[rows, cols] + total[s]) * scale
            value = value.astype(BF16).astype(F32)
            for g in range(halves):
                proj[s * halves + g, pl.ds(8 + r * tile, tile), :] = value[:, g * LANES : (g + 1) * LANES]
    head = lax.broadcasted_iota(jnp.int32, (SUBS, LANES), 0) == 0
    for g in range(width // LANES):
        lanes = slice(g * LANES, (g + 1) * LANES)

        def strided(s, t):
            return proj[s * halves + g, pl.ds(8 + t, SUBS, stride=chunk), :]

        def step(t, carry, masked):
            windows, states = carry
            short = []
            moved = []
            for s in range(3):
                newest = strided(s, t)
                line = windows[s] + [newest]
                value = None
                for j in range(SPAN):
                    at = (j * 3 + s) * SUBS
                    term = taps[at : at + SUBS, lanes] * line[REACH - j]
                    value = term if value is None else value + term
                short.append(value)
                moved.append(line[1:])
            kv = (short[1] * short[2]).astype(BF16).astype(F32)
            if masked:
                kv = jnp.where(head, 0.0, kv)
            out = None
            later = []
            for n in range(MODES):
                at = n * SUBS
                state = decay[at : at + SUBS, lanes] * states[n] + kv
                later.append(state)
                term = weight[at : at + SUBS, lanes] * state
                out = term if out is None else out + term
            place = pl.ds(pl.multiple_of(t * SUBS, SUBS), SUBS)
            gate[place, lanes] = short[0].astype(BF16).astype(F32)
            local[place, lanes] = out
            return moved, later

        windows = [
            [strided(s, t) for t in range(-REACH, 0)]
            for s in range(3)
        ]
        carry = (windows, [jnp.zeros((SUBS, LANES), F32)] * MODES)
        unroll = 8
        for t in range(unroll):
            carry = step(t, carry, t < REACH)

        def steps(i, carry):
            for u in range(unroll):
                carry = step(i * unroll + u, carry, False)
            return carry

        carry = lax.fori_loop(1, chunk // unroll, steps, carry)
        place = lax.broadcasted_iota(jnp.int32, (SUBS, LANES), 0)
        for n in range(MODES):
            at = n * SUBS
            state = carry[1][n]
            for level, hop in enumerate((1, 2, 4)):
                moved = jnp.where(place >= hop, pltpu.roll(state, hop, 0), 0.0)
                jump = jumps[level * MODES + n : level * MODES + n + 1, lanes]
                state = state + jump * moved
            before[at : at + SUBS, lanes] = jnp.where(place >= 1, pltpu.roll(state, 1, 0), 0.0)
            last[n : n + 1, lanes] = state[SUBS - 1 : SUBS, :]
    high = last[...].astype(BF16)
    low = (last[...] - high.astype(F32)).astype(BF16)
    ends = [high, low]
    for s in range(3):
        sides = []
        for g in range(halves):
            tail = proj[s * halves + g, rows_all : rows_all + 8, :]
            sides.append(jnp.concatenate([tail, proj[s * halves + g, 8:16, :]], axis=0))
        ends.append(jnp.concatenate(sides, axis=1).astype(BF16))
    for i, value in enumerate(ends):
        for d in range(8):
            load[d, i * 16 : (i + 1) * 16, :] = value


def join_kernel(chunk, *refs):
    loads, gate, local, before, table, mixed, held, whole, start = refs
    names = ("taps", "decay", "weight", "power", "power_less", "ahead", "early", "late")
    taps, decay, weight, power, power_less, ahead, early, late = (part(table, n) for n in names)
    step_rows = 64
    width = mixed.shape[1]
    me = lax.axis_index("ctx")
    for d in range(9):
        source = jnp.maximum(me - d, 0)
        value = None
        if d < 8:
            value = loads[source].astype(F32)
            value = jnp.concatenate([value[0:16] + value[16:32], value[32:]], axis=0)
            value = jnp.where(me >= d, value, 0.0)
        for g in range(width // LANES):
            piece = jnp.zeros((step_rows, LANES), F32)
            if d < 8:
                piece = value[:, g * LANES : (g + 1) * LANES]
            held[g, d * step_rows : (d + 1) * step_rows, :] = piece
    place = lax.broadcasted_iota(jnp.int32, (SUBS, LANES), 0)
    head = place == 0
    for g in range(width // LANES):
        lanes = slice(g * LANES, (g + 1) * LANES)

        def strided(row):
            return held[g, pl.ds(row, SUBS, stride=step_rows), :]

        short = []
        for s in range(3):
            line = [strided(step_rows + 16 + s * 16 + 8 - REACH + t) for t in range(REACH)]
            line += [strided(24 + s * 16 + t) for t in range(REACH)]
            values = []
            for t in range(REACH):
                value = None
                for j in range(SPAN):
                    at = (j * 3 + s) * SUBS
                    term = taps[at : at + SUBS, lanes] * line[REACH + t - j]
                    value = term if value is None else value + term
                values.append(value)
            short.append(values)
        kv = [(short[1][t] * short[2][t]).astype(BF16).astype(F32) for t in range(REACH)]
        q = [short[0][t].astype(BF16).astype(F32) for t in range(REACH)]
        for n in range(MODES):
            at = n * SUBS
            full = strided(n)
            own = None
            for t in range(REACH):
                row = t * MODES + n
                full = full + late[row : row + 1, lanes] * kv[t]
                term = early[row : row + 1, lanes] * kv[t]
                own = term if own is None else own + term
            arrived = jnp.sum(ahead[at : at + SUBS, lanes] * full, axis=0, keepdims=True)
            state = before[at : at + SUBS, lanes] + power[at : at + SUBS, lanes] * arrived
            state = state + power_less[at : at + SUBS, lanes] * own[0:1, :]
            start[at : at + SUBS, lanes] = state * weight[at : at + SUBS, lanes]

        def step(t, states, extra, fixed):
            out = None
            later = []
            for n in range(MODES):
                at = n * SUBS
                state = decay[at : at + SUBS, lanes] * states[n]
                if extra is not None:
                    state = state + weight[at : at + SUBS, lanes] * extra
                later.append(state)
                out = state if out is None else out + state
            rows = pl.ds(pl.multiple_of(t * SUBS, SUBS), SUBS)
            q_now = gate[rows, lanes]
            if fixed is not None:
                q_now = jnp.where(head, fixed, q_now)
            whole[g, pl.ds(t, SUBS, stride=chunk), :] = q_now * (out + local[rows, lanes])
            return later

        states = [start[n * SUBS : (n + 1) * SUBS, lanes] for n in range(MODES)]
        unroll = 8
        for t in range(unroll):
            first = t < REACH
            extra = jnp.where(head, kv[t], 0.0) if first else None
            states = step(t, states, extra, q[t] if first else None)

        def steps(i, states):
            for u in range(unroll):
                states = step(i * unroll + u, states, None, None)
            return states

        lax.fori_loop(1, chunk // unroll, steps, states)
    for g in range(width // LANES):
        mixed[:, g * LANES : (g + 1) * LANES] = whole[g].astype(BF16)


def out_kernel(begin, layout, fresh, last, w, *refs):
    count = 1 + max(p[0] for p in layout)
    pieces = refs[:count]
    rest = list(refs[count:])
    acc_in = None if fresh else rest.pop(0)
    tokens = rest.pop(0) if last else None
    out = rest.pop(0)
    tile = TILE
    for r in range(out.shape[0] // tile):
        rows = pl.ds(r * tile, tile)
        total = None if fresh else acc_in[rows, :]
        x = jnp.concatenate([piece_rows(pieces, p, r, tile) for p in layout], axis=1)
        some = slice(begin * 256, (begin + len(layout)) * 256)
        product = jnp.dot(x, w[some, :], preferred_element_type=F32)
        total = product if fresh else total + product
        if last:
            total = total + tokens[rows, :].astype(F32)
        out[rows, :] = total.astype(out.dtype)


def out_project(length, begin, pieces, w, state, tokens=None):
    layout, flat = number(pieces)
    rows = length
    last = tokens is not None
    ins = [w] + flat + ([] if state is None else [state]) + ([tokens] if last else [])

    def kernel(*refs):
        out_kernel(begin, layout, state is None, last, *refs)

    outs = jax.ShapeDtypeStruct((rows, 256), BF16 if last else F32)
    aliases = {1 + len(flat): 0} if (state is not None and not last) else {}
    return call(
        kernel, outs, ins, [VMEM] * len(ins), [], 12, len(pieces) * 2 * rows * 256 * 256, aliases
    )


def shifted(x, dy, dz, dc):
    pairs = []
    for i in range(16):
        y, z, c = i // 4, (i // 2) % 2, i % 2
        pairs.append((i, ((y + dy) % 4) * 4 + ((z + dz) % 2) * 2 + (c + dc) % 2))
    return lax.ppermute(x, "tp", pairs)


def tie(value, *others):
    return lax.optimization_barrier((value,) + others)[0]


def body(tokens, norm_gain, w_in, w_short, decay_rate, residue, w_out):
    length, chans = tokens.shape
    half = length // 2
    chunk = length // SUBS

    def other(p, *after):
        return shifted(tie(p, *after) if after else p, 0, 0, 1)

    def gather(x, start, add):
        up = shifted(x, 0, 1, 0)
        far = shifted(x, 2, 0, 0)
        x_other = other(x)
        if start is not None:
            x_other = tie(x_other, start)
        state, mark = add(0, [x, x_other], None)
        up, far, mark = lax.optimization_barrier((up, far, mark))
        both = jnp.concatenate([x, up], axis=0)
        left = shifted(both, 1, 0, 0)
        right = shifted(both, -1, 0, 0)
        up_far = shifted(far, 0, 1, 0)
        up_other, far_other = other(up), other(far)
        state, mark = add(2, [up, up_other, far, far_other], state)
        up_far, left, right, mark = lax.optimization_barrier((up_far, left, right, mark))
        up_far_other, left_other, right_other = other(up_far), other(left), other(right)
        state, mark = add(6, [up_far, left, (left, length), right, (right, length)], state)
        state, mark = add(11, [up_far_other, left_other, (left_other, length)], state)
        return [right_other, (right_other, length)], state

    width = chans

    def prepare():
        def kernel(*refs):
            order_kernel(chunk, *refs)

        return pl.pallas_call(
            kernel,
            out_shape=[
                jax.ShapeDtypeStruct((3, 16 * width, width), BF16),
                jax.ShapeDtypeStruct((16 * width, width), BF16),
                jax.ShapeDtypeStruct((16, width), F32),
                jax.ShapeDtypeStruct((TABLE_ROWS, width), F32),
            ],
            in_specs=[HBM, HBM] + [VMEM] * 4,
            out_specs=[VMEM] * 4,
            scratch_shapes=[pltpu.SemaphoreType.DMA((2, 16))],
            compiler_params=pltpu.CompilerParams(vmem_limit_bytes=4 * MIB),
            cost_estimate=pl.CostEstimate(flops=1, bytes_accessed=1, transcendentals=0),
        )(
            w_in.transpose(1, 0, 2),
            w_out,
            norm_gain.reshape(16, width),
            decay_rate.T,
            residue.T,
            w_short.reshape(SPAN * 3, width),
        )

    first, second, gain, table = prepare()

    def add_in(begin, pieces, state):
        state = project(length, begin, pieces, gain, first, state)
        return state, state[0]

    pieces, state = gather(tokens, table, add_in)
    layout, flat = number(pieces)
    ins = [gain, first] + flat + list(state) + [table]

    def kernel(*refs):
        local_kernel(14, layout, chunk, *refs)

    gate, local, before, load = call(
        kernel,
        [
            jax.ShapeDtypeStruct((length, chans), F32),
            jax.ShapeDtypeStruct((length, chans), F32),
            jax.ShapeDtypeStruct((MODES * SUBS, chans), F32),
            jax.ShapeDtypeStruct((8, 80, chans), BF16),
        ],
        ins,
        [VMEM] * len(ins),
        [
            pltpu.VMEM((3 * chans // LANES, length + 8, LANES), F32),
            pltpu.VMEM((MODES, chans), F32),
        ],
        20,
        4 * 10**9,
    )
    loads = lax.all_to_all(load, "ctx", 0, 0, tiled=True)
    ins = [loads, gate, local, before, table]

    def kernel_two(*refs):
        join_kernel(chunk, *refs)

    mixed = call(
        kernel_two,
        jax.ShapeDtypeStruct((length, chans), BF16),
        ins,
        [VMEM] * len(ins),
        [
            pltpu.VMEM((chans // LANES, 9 * 64, LANES), F32),
            pltpu.VMEM((chans // LANES, length, LANES), F32),
            pltpu.VMEM((MODES * SUBS, chans), F32),
        ],
        12,
        2 * 10**9,
    )

    def add_out(begin, pieces, state):
        state = out_project(length, begin, pieces, second, state)
        return state, state

    pieces, state = gather(mixed, None, add_out)
    return out_project(length, 14, pieces, second, state, tokens)


def solution(mesh):
    placed = (
        P("ctx", "tp"),
        P(),
        P(None, None, "tp"),
        P(None, None, "tp"),
        P("tp", None),
        P("tp", None),
        P(None, "tp"),
    )
    return jax.shard_map(
        body, mesh=mesh, in_specs=placed, out_specs=P("ctx", "tp"), check_vma=False
    )
```

```python
import jax
import jax.numpy as jnp
from jax import lax
from jax.experimental import pallas as pl
from jax.experimental.pallas import tpu as pltpu
from jax.sharding import PartitionSpec as P

F32 = jnp.float32
BF16 = jnp.bfloat16
MODES = 16
SPAN = 7
REACH = SPAN - 1
LANES = 128
SUBS = 8
VMEM = pl.BlockSpec(memory_space=pltpu.VMEM)
HBM = pl.BlockSpec(memory_space=pltpu.HBM)
SMEM = pl.BlockSpec(memory_space=pltpu.SMEM)
MIB = 1024 * 1024
TILE = 512


def call(kernel, outs, ins, specs, scratch, limit, aliases=None):
    return pl.pallas_call(
        kernel,
        out_shape=outs,
        in_specs=specs,
        out_specs=[VMEM] * len(outs) if isinstance(outs, list) else VMEM,
        scratch_shapes=scratch,
        input_output_aliases=aliases or {},
        compiler_params=pltpu.CompilerParams(vmem_limit_bytes=limit * MIB),
        cost_estimate=pl.CostEstimate(flops=1, bytes_accessed=1, transcendentals=0),
    )(*ins)


TABLE = {}
for _name, _rows in (
    ("decay", MODES * SUBS),
    ("weight", MODES * SUBS),
    ("power", MODES * SUBS),
    ("power_less", MODES * SUBS),
    ("ahead", MODES * SUBS),
    ("taps", SPAN * 3 * SUBS),
    ("jumps", 3 * MODES),
    ("early", REACH * MODES),
    ("late", REACH * MODES),
):
    TABLE[_name] = (sum(rows for _, rows in TABLE.values()), _rows)
TABLE_ROWS = sum(rows for _, rows in TABLE.values())

def part(table, name):
    begin, rows = TABLE[name]
    return table.at[pl.ds(begin, rows)]


def source(place):
    me = lax.axis_index("tp")
    y, z, c = me // 4, (me // 2) % 2, me % 2
    dy, dz, dc = place
    return ((y + dy + 4) % 4) * 4 + ((z + dz) % 2) * 2 + (c + dc) % 2


def table_kernel(chunk, rate, residue, short, table):
    width = table.shape[1]
    length = SUBS * chunk
    sub = lax.broadcasted_iota(jnp.int32, (SUBS, width), 0)
    lag = sub.astype(F32)

    def put(name, row, value):
        at = TABLE[name][0] + row
        table[at : at + value.shape[0], :] = value

    rates = rate[...]
    for level, hop in enumerate((1, 2, 4)):
        put("jumps", level * MODES, jnp.exp(-rates * (chunk * hop)))
    for t in range(REACH):
        put("early", t * MODES, jnp.exp(-rates * (chunk - 1 - t)))
        put("late", t * MODES, jnp.exp(-rates * (length - 1 - t)))
    weights = residue[...] * jnp.sqrt(rates)
    decays = jnp.exp(-rates)
    for n in range(MODES):
        wide = jnp.broadcast_to(rates[n : n + 1, :], (SUBS, width))
        put("decay", n * SUBS, jnp.broadcast_to(decays[n : n + 1, :], (SUBS, width)))
        put("weight", n * SUBS, jnp.broadcast_to(weights[n : n + 1, :], (SUBS, width)))
        put("power", n * SUBS, jnp.exp(-wide * (lag * chunk)))
        less = jnp.exp(-wide * (jnp.maximum(lag - 1.0, 0.0) * chunk))
        put("power_less", n * SUBS, jnp.where(sub >= 1, less, 0.0))
        far = jnp.exp(-wide * (jnp.maximum(lag - 1.0, 0.0) * length))
        put("ahead", n * SUBS, jnp.where(sub >= 1, far, 0.0))
    for i in range(SPAN * 3):
        tap = short[i // 3, i % 3 : i % 3 + 1, :]
        put("taps", i * SUBS, jnp.broadcast_to(tap, (SUBS, width)))


def add_pieces(layout, gain, w, refs, r, tile):
    squares = None
    scaled = []
    blocks = []
    for number, first, place in layout:
        block = source(place)
        x = refs[number][pl.ds(first + r * tile, tile), :].astype(F32)
        scaled.append((x * gain[pl.ds(block, 1), :]).astype(BF16))
        square = x * x
        square = square[:, :LANES] + square[:, LANES:]
        squares = square if squares is None else squares + square
        blocks.append(pl.ds(pl.multiple_of(block * 256, 256), 256))
    scaled = jnp.concatenate(scaled, axis=1)
    total = []
    for s in range(3):
        weights = jnp.concatenate([w[s, rows, :] for rows in blocks], axis=0)
        total.append(jnp.dot(scaled, weights, preferred_element_type=F32))
    return total, squares


def proj_kernel(layout, fresh, gain, w, *refs):
    count = 1 + max(p[0] for p in layout)
    pieces = refs[:count]
    if fresh:
        acc, ss = refs[count:]
    else:
        acc_in, ss_in, acc, ss = refs[count:]
    tile = TILE
    for r in range(acc.shape[0] // tile):
        rows = pl.ds(r * tile, tile)
        total, squares = add_pieces(layout, gain, w, pieces, r, tile)
        for s in range(3):
            cols = slice(s * 256, (s + 1) * 256)
            acc[rows, cols] = total[s] if fresh else acc_in[rows, cols] + total[s]
        ss[rows, :] = squares if fresh else ss_in[rows, :] + squares


def number(pieces):
    layout, flat = [], []
    for array, first, place in pieces:
        known = [i for i, a in enumerate(flat) if a is array]
        if not known:
            flat.append(array)
        layout.append((known[0] if known else len(flat) - 1, first, place))
    return layout, flat


def project(length, pieces, gain, w, state):
    layout, flat = number(pieces)
    rows = length
    outs = [jax.ShapeDtypeStruct((rows, 768), F32), jax.ShapeDtypeStruct((rows, LANES), F32)]
    ins = [gain, w] + flat + (list(state) if state else [])
    specs = [VMEM] * len(ins)
    fresh = state is None

    def kernel(*refs):
        proj_kernel(layout, fresh, *refs)

    aliases = {} if fresh else {len(ins) - 2: 0, len(ins) - 1: 1}
    return call(kernel, outs, ins, specs, [], 16, aliases)


def local_kernel(layout, chunk, gain, w, *refs):
    count = 1 + max(p[0] for p in layout)
    pieces = refs[:count]
    acc, ss, table, gate, local, before, load, proj, last = refs[count:]
    taps, decay, weight, jumps = (part(table, n) for n in ("taps", "decay", "weight", "jumps"))
    tile = TILE
    width = gate.shape[1]
    rows_all = acc.shape[0]
    halves = width // LANES
    proj[:, 0:8, :] = jnp.zeros((3 * halves, 8, LANES), F32)
    for r in range(rows_all // tile):
        rows = pl.ds(r * tile, tile)
        total, squares = add_pieces(layout, gain, w, pieces, r, tile)
        mean = jnp.sum(ss[rows, :] + squares, axis=1, keepdims=True) / (16 * width)
        scale = lax.rsqrt(mean + 1e-05)
        for s in range(3):
            cols = slice(s * 256, (s + 1) * 256)
            value = (acc[rows, cols] + total[s]) * scale
            value = value.astype(BF16).astype(F32)
            for g in range(halves):
                proj[s * halves + g, pl.ds(8 + r * tile, tile), :] = value[:, g * LANES : (g + 1) * LANES]
    head = lax.broadcasted_iota(jnp.int32, (SUBS, LANES), 0) == 0
    for g in range(width // LANES):
        lanes = slice(g * LANES, (g + 1) * LANES)

        def strided(s, t):
            return proj[s * halves + g, pl.ds(8 + t, SUBS, stride=chunk), :]

        def step(t, carry, masked):
            windows, states = carry
            short = []
            moved = []
            for s in range(3):
                newest = strided(s, t)
                line = windows[s] + [newest]
                value = None
                for j in range(SPAN):
                    at = (j * 3 + s) * SUBS
                    term = taps[at : at + SUBS, lanes] * line[REACH - j]
                    value = term if value is None else value + term
                short.append(value)
                moved.append(line[1:])
            kv = (short[1] * short[2]).astype(BF16).astype(F32)
            if masked:
                kv = jnp.where(head, 0.0, kv)
            out = None
            later = []
            for n in range(MODES):
                at = n * SUBS
                state = decay[at : at + SUBS, lanes] * states[n] + kv
                later.append(state)
                term = weight[at : at + SUBS, lanes] * state
                out = term if out is None else out + term
            place = pl.ds(pl.multiple_of(t * SUBS, SUBS), SUBS)
            gate[place, lanes] = short[0].astype(BF16).astype(F32)
            local[place, lanes] = out
            return moved, later

        windows = [
            [strided(s, t) for t in range(-REACH, 0)]
            for s in range(3)
        ]
        carry = (windows, [jnp.zeros((SUBS, LANES), F32)] * MODES)
        unroll = 8
        for t in range(unroll):
            carry = step(t, carry, t < REACH)

        def steps(i, carry):
            for u in range(unroll):
                carry = step(i * unroll + u, carry, False)
            return carry

        carry = lax.fori_loop(1, chunk // unroll, steps, carry)
        place = lax.broadcasted_iota(jnp.int32, (SUBS, LANES), 0)
        for n in range(MODES):
            at = n * SUBS
            state = carry[1][n]
            for level, hop in enumerate((1, 2, 4)):
                moved = jnp.where(place >= hop, pltpu.roll(state, hop, 0), 0.0)
                jump = jumps[level * MODES + n : level * MODES + n + 1, lanes]
                state = state + jump * moved
            before[at : at + SUBS, lanes] = jnp.where(place >= 1, pltpu.roll(state, 1, 0), 0.0)
            last[n : n + 1, lanes] = state[SUBS - 1 : SUBS, :]
    high = last[...].astype(BF16)
    low = (last[...] - high.astype(F32)).astype(BF16)
    ends = [high, low]
    for s in range(3):
        sides = []
        for g in range(halves):
            tail = proj[s * halves + g, rows_all : rows_all + 8, :]
            sides.append(jnp.concatenate([tail, proj[s * halves + g, 8:16, :]], axis=0))
        ends.append(jnp.concatenate(sides, axis=1).astype(BF16))
    for i, value in enumerate(ends):
        for d in range(8):
            load[d, i * 16 : (i + 1) * 16, :] = value


def join_kernel(chunk, *refs):
    loads, gate, local, before, table, mixed, held, whole, start = refs
    names = ("taps", "decay", "weight", "power", "power_less", "ahead", "early", "late")
    taps, decay, weight, power, power_less, ahead, early, late = (part(table, n) for n in names)
    step_rows = 64
    width = mixed.shape[1]
    me = lax.axis_index("ctx")
    for d in range(9):
        source = jnp.maximum(me - d, 0)
        value = None
        if d < 8:
            value = loads[source].astype(F32)
            value = jnp.concatenate([value[0:16] + value[16:32], value[32:]], axis=0)
            value = jnp.where(me >= d, value, 0.0)
        for g in range(width // LANES):
            piece = jnp.zeros((step_rows, LANES), F32)
            if d < 8:
                piece = value[:, g * LANES : (g + 1) * LANES]
            held[g, d * step_rows : (d + 1) * step_rows, :] = piece
    place = lax.broadcasted_iota(jnp.int32, (SUBS, LANES), 0)
    head = place == 0
    for g in range(width // LANES):
        lanes = slice(g * LANES, (g + 1) * LANES)

        def strided(row):
            return held[g, pl.ds(row, SUBS, stride=step_rows), :]

        short = []
        for s in range(3):
            line = [strided(step_rows + 16 + s * 16 + 8 - REACH + t) for t in range(REACH)]
            line += [strided(24 + s * 16 + t) for t in range(REACH)]
            values = []
            for t in range(REACH):
                value = None
                for j in range(SPAN):
                    at = (j * 3 + s) * SUBS
                    term = taps[at : at + SUBS, lanes] * line[REACH + t - j]
                    value = term if value is None else value + term
                values.append(value)
            short.append(values)
        kv = [(short[1][t] * short[2][t]).astype(BF16).astype(F32) for t in range(REACH)]
        q = [short[0][t].astype(BF16).astype(F32) for t in range(REACH)]
        for n in range(MODES):
            at = n * SUBS
            full = strided(n)
            own = None
            for t in range(REACH):
                row = t * MODES + n
                full = full + late[row : row + 1, lanes] * kv[t]
                term = early[row : row + 1, lanes] * kv[t]
                own = term if own is None else own + term
            arrived = jnp.sum(ahead[at : at + SUBS, lanes] * full, axis=0, keepdims=True)
            state = before[at : at + SUBS, lanes] + power[at : at + SUBS, lanes] * arrived
            state = state + power_less[at : at + SUBS, lanes] * own[0:1, :]
            start[at : at + SUBS, lanes] = state * weight[at : at + SUBS, lanes]

        def step(t, states, extra, fixed):
            out = None
            later = []
            for n in range(MODES):
                at = n * SUBS
                state = decay[at : at + SUBS, lanes] * states[n]
                if extra is not None:
                    state = state + weight[at : at + SUBS, lanes] * extra
                later.append(state)
                out = state if out is None else out + state
            rows = pl.ds(pl.multiple_of(t * SUBS, SUBS), SUBS)
            q_now = gate[rows, lanes]
            if fixed is not None:
                q_now = jnp.where(head, fixed, q_now)
            whole[g, pl.ds(t, SUBS, stride=chunk), :] = q_now * (out + local[rows, lanes])
            return later

        states = [start[n * SUBS : (n + 1) * SUBS, lanes] for n in range(MODES)]
        unroll = 8
        for t in range(unroll):
            first = t < REACH
            extra = jnp.where(head, kv[t], 0.0) if first else None
            states = step(t, states, extra, q[t] if first else None)

        def steps(i, states):
            for u in range(unroll):
                states = step(i * unroll + u, states, None, None)
            return states

        lax.fori_loop(1, chunk // unroll, steps, states)
    for g in range(width // LANES):
        mixed[:, g * LANES : (g + 1) * LANES] = whole[g].astype(BF16)


def out_kernel(layout, fresh, last, w, *refs):
    count = 1 + max(p[0] for p in layout)
    pieces = refs[:count]
    rest = list(refs[count:])
    acc_in = None if fresh else rest.pop(0)
    tokens = rest.pop(0) if last else None
    out = rest.pop(0)
    tile = TILE
    for r in range(out.shape[0] // tile):
        rows = pl.ds(r * tile, tile)
        total = None if fresh else acc_in[rows, :]
        parts, weights = [], []
        for number, first, place in layout:
            parts.append(pieces[number][pl.ds(first + r * tile, tile), :])
            weights.append(w[pl.ds(pl.multiple_of(source(place) * 256, 256), 256), :])
        product = jnp.dot(
            jnp.concatenate(parts, axis=1),
            jnp.concatenate(weights, axis=0),
            preferred_element_type=F32,
        )
        total = product if fresh else total + product
        if last:
            total = total + tokens[rows, :].astype(F32)
        out[rows, :] = total.astype(out.dtype)


def out_project(length, pieces, w, state, tokens=None):
    layout, flat = number(pieces)
    rows = length
    last = tokens is not None
    ins = [w] + flat + ([] if state is None else [state]) + ([tokens] if last else [])

    def kernel(*refs):
        out_kernel(layout, state is None, last, *refs)

    outs = jax.ShapeDtypeStruct((rows, 256), BF16 if last else F32)
    aliases = {1 + len(flat): 0} if (state is not None and not last) else {}
    return call(
        kernel, outs, ins, [VMEM] * len(ins), [], 12, aliases
    )


def shifted(x, dy, dz, dc):
    pairs = []
    for i in range(16):
        y, z, c = i // 4, (i // 2) % 2, i % 2
        pairs.append((i, ((y + dy) % 4) * 4 + ((z + dz) % 2) * 2 + (c + dc) % 2))
    return lax.ppermute(x, "tp", pairs)


def tie(value, *others):
    return lax.optimization_barrier((value,) + others)[0]


def body(tokens, norm_gain, w_in, w_short, decay_rate, residue, w_out):
    length, chans = tokens.shape
    half = length // 2
    chunk = length // SUBS

    def other(p, *after):
        return shifted(tie(p, *after) if after else p, 0, 0, 1)

    def gather(x, start, add):
        up = shifted(x, 0, 1, 0)
        far = shifted(x, 2, 0, 0)
        left = shifted(x, 1, 0, 0)
        right = shifted(x, -1, 0, 0)
        x_other = other(x)
        if start is not None:
            x_other = tie(x_other, start)
        state, mark = add([(x, 0, (0, 0, 0)), (x_other, 0, (0, 0, 1))], None)
        up, far, mark = lax.optimization_barrier((up, far, mark))
        up_left = shifted(up, 1, 0, 0)
        up_right = shifted(up, -1, 0, 0)
        up_far = shifted(far, 0, 1, 0)
        up_other, far_other = other(up, left, right), other(far, left, right)
        left_other, right_other = other(left), other(right)
        pieces = [(up, 0, (0, 1, 0)), (far, 0, (2, 0, 0)), (left, 0, (-1, 0, 0)), (right, 0, (1, 0, 0))]
        state, mark = add(pieces, state)
        up_left, up_right, up_far, mark = lax.optimization_barrier((up_left, up_right, up_far, mark))
        up_far_other, up_left_other, up_right_other = other(up_far), other(up_left), other(up_right)
        pieces = [(up_far, 0, (2, 1, 0)), (up_left, 0, (-1, 1, 0)), (up_right, 0, (1, 1, 0))]
        state, mark = add(pieces, state)
        pieces = [(up_other, 0, (0, 1, 1)), (far_other, 0, (2, 0, 1))]
        pieces += [(left_other, 0, (-1, 0, 1)), (right_other, 0, (1, 0, 1))]
        state, mark = add(pieces, state)
        pieces = [(up_far_other, 0, (2, 1, 1)), (up_left_other, 0, (-1, 1, 1))]
        return pieces + [(up_right_other, 0, (1, 1, 1))], state

    width = chans

    table = call(
        lambda *refs: table_kernel(chunk, *refs),
        jax.ShapeDtypeStruct((TABLE_ROWS, width), F32),
        [decay_rate.T, residue.T, w_short],
        [VMEM] * 3,
        [],
        4,
    )
    gain = norm_gain.reshape(16, width)
    first = w_in.transpose(1, 0, 2)
    second = w_out

    def add_in(pieces, state):
        state = project(length, pieces, gain, first, state)
        return state, state[0]

    pieces, state = gather(tokens, table, add_in)
    layout, flat = number(pieces)
    ins = [gain, first] + flat + list(state) + [table]

    def kernel(*refs):
        local_kernel(layout, chunk, *refs)

    gate, local, before, load = call(
        kernel,
        [
            jax.ShapeDtypeStruct((length, chans), F32),
            jax.ShapeDtypeStruct((length, chans), F32),
            jax.ShapeDtypeStruct((MODES * SUBS, chans), F32),
            jax.ShapeDtypeStruct((8, 80, chans), BF16),
        ],
        ins,
        [VMEM] * len(ins),
        [
            pltpu.VMEM((3 * chans // LANES, length + 8, LANES), F32),
            pltpu.VMEM((MODES, chans), F32),
        ],
        20,
    )
    loads = lax.all_to_all(load, "ctx", 0, 0, tiled=True)
    ins = [loads, gate, local, before, table]

    def kernel_two(*refs):
        join_kernel(chunk, *refs)

    mixed = call(
        kernel_two,
        jax.ShapeDtypeStruct((length, chans), BF16),
        ins,
        [VMEM] * len(ins),
        [
            pltpu.VMEM((chans // LANES, 9 * 64, LANES), F32),
            pltpu.VMEM((chans // LANES, length, LANES), F32),
            pltpu.VMEM((MODES * SUBS, chans), F32),
        ],
        12,
    )

    def add_out(pieces, state):
        state = out_project(length, pieces, second, state)
        return state, state

    pieces, state = gather(mixed, None, add_out)
    return out_project(length, pieces, second, state, tokens)


def solution(mesh):
    placed = (
        P("ctx", "tp"),
        P(),
        P(None, None, "tp"),
        P(None, None, "tp"),
        P("tp", None),
        P("tp", None),
        P(None, "tp"),
    )
    return jax.shard_map(
        body, mesh=mesh, in_specs=placed, out_specs=P("ctx", "tp"), check_vma=False
    )
```

```python
import jax
import jax.numpy as jnp
from jax import lax
from jax.experimental import pallas as pl
from jax.experimental.pallas import tpu as pltpu
from jax.sharding import PartitionSpec as P

F32 = jnp.float32
BF16 = jnp.bfloat16
MODES = 16
SPAN = 7
REACH = SPAN - 1
LANES = 128
SUBS = 8
VMEM = pl.BlockSpec(memory_space=pltpu.VMEM)
HBM = pl.BlockSpec(memory_space=pltpu.HBM)
SMEM = pl.BlockSpec(memory_space=pltpu.SMEM)
MIB = 1024 * 1024
TILE = 512
GROUP = 4
PAD = 8


def call(kernel, outs, ins, specs, scratch, limit, aliases=None):
    return pl.pallas_call(
        kernel,
        out_shape=outs,
        in_specs=specs,
        out_specs=[VMEM] * len(outs) if isinstance(outs, list) else VMEM,
        scratch_shapes=scratch,
        input_output_aliases=aliases or {},
        compiler_params=pltpu.CompilerParams(vmem_limit_bytes=limit * MIB),
        cost_estimate=pl.CostEstimate(flops=1, bytes_accessed=1, transcendentals=0),
    )(*ins)


TABLE = {}
for _name, _rows in (
    ("decay", MODES * SUBS),
    ("weight", MODES * SUBS),
    ("power", MODES * SUBS),
    ("power_less", MODES * SUBS),
    ("ahead", MODES * SUBS),
    ("taps", SPAN * 3 * SUBS),
    ("jumps", 3 * MODES),
    ("early", REACH * MODES),
    ("late", REACH * MODES),
):
    TABLE[_name] = (sum(rows for _, rows in TABLE.values()), _rows)
TABLE_ROWS = sum(rows for _, rows in TABLE.values())

def add_up(terms):
    while len(terms) > 1:
        terms = [a + b for a, b in zip(terms[::2], terms[1::2])] + terms[len(terms) & ~1 :]
    return terms[0]


def part(table, name):
    begin, rows = TABLE[name]
    return table.at[pl.ds(begin, rows)]


def source(place):
    me = lax.axis_index("tp")
    y, z, c = me // 4, (me // 2) % 2, me % 2
    dy, dz, dc = place
    return ((y + dy + 4) % 4) * 4 + ((z + dz) % 2) * 2 + (c + dc) % 2


def table_kernel(chunk, rate, residue, short, table):
    width = table.shape[1]
    length = SUBS * chunk
    sub = lax.broadcasted_iota(jnp.int32, (SUBS, width), 0)
    lag = sub.astype(F32)

    def put(name, row, value):
        at = TABLE[name][0] + row
        table[at : at + value.shape[0], :] = value

    rates = rate[...]
    for level, hop in enumerate((1, 2, 4)):
        put("jumps", level * MODES, jnp.exp(-rates * (chunk * hop)))
    for t in range(REACH):
        put("early", t * MODES, jnp.exp(-rates * (chunk - 1 - t)))
        put("late", t * MODES, jnp.exp(-rates * (length - 1 - t)))
    weights = residue[...] * jnp.sqrt(rates)
    decays = jnp.exp(-rates)
    for n in range(MODES):
        wide = jnp.broadcast_to(rates[n : n + 1, :], (SUBS, width))
        put("decay", n * SUBS, jnp.broadcast_to(decays[n : n + 1, :], (SUBS, width)))
        put("weight", n * SUBS, jnp.broadcast_to(weights[n : n + 1, :], (SUBS, width)))
        put("power", n * SUBS, jnp.exp(-wide * (lag * chunk)))
        less = jnp.exp(-wide * (jnp.maximum(lag - 1.0, 0.0) * chunk))
        put("power_less", n * SUBS, jnp.where(sub >= 1, less, 0.0))
        far = jnp.exp(-wide * (jnp.maximum(lag - 1.0, 0.0) * length))
        put("ahead", n * SUBS, jnp.where(sub >= 1, far, 0.0))
    for i in range(SPAN * 3):
        tap = short[i // 3, i % 3 : i % 3 + 1, :]
        put("taps", i * SUBS, jnp.broadcast_to(tap, (SUBS, width)))


def add_pieces(layout, gain, w, refs, r, tile):
    squares = None
    scaled = []
    blocks = []
    for number, first, place in layout:
        block = source(place)
        x = refs[number][pl.ds(first + r * tile, tile), :].astype(F32)
        scaled.append((x * gain[pl.ds(block, 1), :]).astype(BF16))
        square = x * x
        square = square[:, :LANES] + square[:, LANES:]
        squares = square if squares is None else squares + square
        blocks.append(pl.ds(pl.multiple_of(block * 256, 256), 256))
    scaled = jnp.concatenate(scaled, axis=1)
    total = []
    for s in range(3):
        weights = jnp.concatenate([w[s, rows, :] for rows in blocks], axis=0)
        total.append(jnp.dot(scaled, weights, preferred_element_type=F32))
    return total, squares


def proj_kernel(layout, fresh, gain, w, *refs):
    count = 1 + max(p[0] for p in layout)
    pieces = refs[:count]
    if fresh:
        acc, ss = refs[count:]
    else:
        acc_in, ss_in, acc, ss = refs[count:]
    tile = TILE
    for r in range(acc.shape[0] // tile):
        rows = pl.ds(r * tile, tile)
        total, squares = add_pieces(layout, gain, w, pieces, r, tile)
        for s in range(3):
            cols = slice(s * 256, (s + 1) * 256)
            acc[rows, cols] = total[s] if fresh else acc_in[rows, cols] + total[s]
        ss[rows, :] = squares if fresh else ss_in[rows, :] + squares


def number(pieces):
    layout, flat = [], []
    for array, first, place in pieces:
        known = [i for i, a in enumerate(flat) if a is array]
        if not known:
            flat.append(array)
        layout.append((known[0] if known else len(flat) - 1, first, place))
    return layout, flat


def project(length, pieces, gain, w, state):
    layout, flat = number(pieces)
    rows = length
    outs = [jax.ShapeDtypeStruct((rows, 768), F32), jax.ShapeDtypeStruct((rows, LANES), F32)]
    ins = [gain, w] + flat + (list(state) if state else [])
    specs = [VMEM] * len(ins)
    fresh = state is None

    def kernel(*refs):
        proj_kernel(layout, fresh, *refs)

    aliases = {} if fresh else {len(ins) - 2: 0, len(ins) - 1: 1}
    return call(kernel, outs, ins, specs, [], 16, aliases)


def local_kernel(layout, chunk, gain, w, *refs):
    count = 1 + max(p[0] for p in layout)
    pieces = refs[:count]
    acc, ss, table, gate, local, before, load, proj, last = refs[count:]
    taps, decay, weight, jumps = (part(table, n) for n in ("taps", "decay", "weight", "jumps"))
    tile = TILE
    width = gate.shape[1]
    rows_all = acc.shape[0]
    halves = width // LANES
    pitch = chunk + PAD
    proj[:, 0:PAD, :] = jnp.zeros((3 * halves, PAD, LANES), F32)
    for r in range(rows_all // tile):
        rows = pl.ds(r * tile, tile)
        total, squares = add_pieces(layout, gain, w, pieces, r, tile)
        mean = jnp.sum(ss[rows, :] + squares, axis=1, keepdims=True) / (16 * width)
        scale = lax.rsqrt(mean + 1e-05)
        for s in range(3):
            cols = slice(s * 256, (s + 1) * 256)
            value = (acc[rows, cols] + total[s]) * scale
            value = value.astype(BF16).astype(F32)
            for g in range(halves):
                for k in range(tile // chunk):
                    run = r * (tile // chunk) + k
                    piece = value[k * chunk : (k + 1) * chunk, g * LANES : (g + 1) * LANES]
                    proj[s * halves + g, pl.ds(run * pitch + PAD, chunk), :] = piece
                    if run + 1 < SUBS:
                        proj[s * halves + g, pl.ds((run + 1) * pitch, PAD), :] = piece[chunk - PAD :]
    head = lax.broadcasted_iota(jnp.int32, (SUBS, LANES), 0) == 0
    for g in range(width // LANES):
        lanes = slice(g * LANES, (g + 1) * LANES)

        def strided(s, t):
            return proj[s * halves + g, pl.ds(PAD + t, SUBS, stride=pitch), :]

        unroll = 8

        def steps(i, states, masked=False):
            begin = i * unroll
            short = []
            for s in range(3):
                rows = [strided(s, begin + u) for u in range(-REACH, unroll)]
                weights = [
                    taps[(j * 3 + s) * SUBS : (j * 3 + s + 1) * SUBS, lanes] for j in range(SPAN)
                ]
                short.append(
                    [
                        add_up([weights[j] * rows[REACH + u - j] for j in range(SPAN)])
                        for u in range(unroll)
                    ]
                )
            kv = [(short[1][u] * short[2][u]).astype(BF16).astype(F32) for u in range(unroll)]
            if masked:
                kv = [jnp.where(head, 0.0, v) if u < REACH else v for u, v in enumerate(kv)]
            outs = [None] * unroll
            later = []
            for first in range(0, MODES, GROUP):
                some = range(first, first + GROUP)
                decays = [decay[n * SUBS : (n + 1) * SUBS, lanes] for n in some]
                weights = [weight[n * SUBS : (n + 1) * SUBS, lanes] for n in some]
                now = [states[n] for n in some]
                for u in range(unroll):
                    now = [decays[k] * now[k] + kv[u] for k in range(GROUP)]
                    term = add_up([weights[k] * now[k] for k in range(GROUP)])
                    outs[u] = term if outs[u] is None else outs[u] + term
                later.extend(now)
            for u in range(unroll):
                place = pl.ds(pl.multiple_of((begin + u) * SUBS, SUBS), SUBS)
                gate[place, lanes] = short[0][u].astype(BF16).astype(F32)
                local[place, lanes] = outs[u]
            return later

        states = steps(0, [jnp.zeros((SUBS, LANES), F32)] * MODES, True)
        states = lax.fori_loop(1, chunk // unroll, steps, states)
        place = lax.broadcasted_iota(jnp.int32, (SUBS, LANES), 0)
        for n in range(MODES):
            at = n * SUBS
            state = states[n]
            for level, hop in enumerate((1, 2, 4)):
                moved = jnp.where(place >= hop, pltpu.roll(state, hop, 0), 0.0)
                jump = jumps[level * MODES + n : level * MODES + n + 1, lanes]
                state = state + jump * moved
            before[at : at + SUBS, lanes] = jnp.where(place >= 1, pltpu.roll(state, 1, 0), 0.0)
            last[n : n + 1, lanes] = state[SUBS - 1 : SUBS, :]
    high = last[...].astype(BF16)
    low = (last[...] - high.astype(F32)).astype(BF16)
    ends = [high, low]
    for s in range(3):
        sides = []
        for g in range(halves):
            tail = proj[s * halves + g, SUBS * pitch - PAD : SUBS * pitch, :]
            sides.append(jnp.concatenate([tail, proj[s * halves + g, PAD : 2 * PAD, :]], axis=0))
        ends.append(jnp.concatenate(sides, axis=1).astype(BF16))
    for i, value in enumerate(ends):
        for d in range(8):
            load[d, i * 16 : (i + 1) * 16, :] = value


def join_kernel(chunk, *refs):
    loads, gate, local, before, table, mixed, held, whole, start = refs
    names = ("taps", "decay", "weight", "power", "power_less", "ahead", "early", "late")
    taps, decay, weight, power, power_less, ahead, early, late = (part(table, n) for n in names)
    step_rows = 64 + PAD
    width = mixed.shape[1]
    me = lax.axis_index("ctx")
    for d in range(9):
        source = jnp.maximum(me - d, 0)
        value = None
        if d < 8:
            value = loads[source].astype(F32)
            value = jnp.concatenate([value[0:16] + value[16:32], value[32:]], axis=0)
            value = jnp.where(me >= d, value, 0.0)
        for g in range(width // LANES):
            piece = jnp.zeros((64, LANES), F32)
            if d < 8:
                piece = value[:, g * LANES : (g + 1) * LANES]
            held[g, d * step_rows : d * step_rows + 64, :] = piece
    place = lax.broadcasted_iota(jnp.int32, (SUBS, LANES), 0)
    head = place == 0
    for g in range(width // LANES):
        lanes = slice(g * LANES, (g + 1) * LANES)

        def strided(row):
            return held[g, pl.ds(row, SUBS, stride=step_rows), :]

        short = []
        for s in range(3):
            line = [strided(step_rows + 16 + s * 16 + 8 - REACH + t) for t in range(REACH)]
            line += [strided(24 + s * 16 + t) for t in range(REACH)]
            values = []
            for t in range(REACH):
                value = None
                for j in range(SPAN):
                    at = (j * 3 + s) * SUBS
                    term = taps[at : at + SUBS, lanes] * line[REACH + t - j]
                    value = term if value is None else value + term
                values.append(value)
            short.append(values)
        kv = [(short[1][t] * short[2][t]).astype(BF16).astype(F32) for t in range(REACH)]
        q = [short[0][t].astype(BF16).astype(F32) for t in range(REACH)]
        for n in range(MODES):
            at = n * SUBS
            full = strided(n)
            own = None
            for t in range(REACH):
                row = t * MODES + n
                full = full + late[row : row + 1, lanes] * kv[t]
                term = early[row : row + 1, lanes] * kv[t]
                own = term if own is None else own + term
            arrived = jnp.sum(ahead[at : at + SUBS, lanes] * full, axis=0, keepdims=True)
            state = before[at : at + SUBS, lanes] + power[at : at + SUBS, lanes] * arrived
            state = state + power_less[at : at + SUBS, lanes] * own[0:1, :]
            start[at : at + SUBS, lanes] = state * weight[at : at + SUBS, lanes]

        decays = [decay[n * SUBS : (n + 1) * SUBS, lanes] for n in range(MODES)]

        def step(t, states, extra, fixed):
            later = []
            for n in range(MODES):
                state = decays[n] * states[n]
                if extra is not None:
                    state = state + weight[n * SUBS : (n + 1) * SUBS, lanes] * extra
                later.append(state)
            out = add_up(later)
            rows = pl.ds(pl.multiple_of(t * SUBS, SUBS), SUBS)
            q_now = gate[rows, lanes]
            if fixed is not None:
                q_now = jnp.where(head, fixed, q_now)
            whole[g, pl.ds(t, SUBS, stride=chunk + PAD), :] = q_now * (out + local[rows, lanes])
            return later

        states = [start[n * SUBS : (n + 1) * SUBS, lanes] for n in range(MODES)]
        unroll = 8
        for t in range(unroll):
            first = t < REACH
            extra = jnp.where(head, kv[t], 0.0) if first else None
            states = step(t, states, extra, q[t] if first else None)

        def steps(i, states):
            for u in range(unroll):
                states = step(i * unroll + u, states, None, None)
            return states

        lax.fori_loop(1, chunk // unroll, steps, states)
    for g in range(width // LANES):
        for k in range(SUBS):
            rows = whole[g, k * (chunk + PAD) : k * (chunk + PAD) + chunk, :]
            mixed[k * chunk : (k + 1) * chunk, g * LANES : (g + 1) * LANES] = rows.astype(BF16)


def out_kernel(layout, fresh, last, w, *refs):
    count = 1 + max(p[0] for p in layout)
    pieces = refs[:count]
    rest = list(refs[count:])
    acc_in = None if fresh else rest.pop(0)
    tokens = rest.pop(0) if last else None
    out = rest.pop(0)
    tile = TILE
    for r in range(out.shape[0] // tile):
        rows = pl.ds(r * tile, tile)
        total = None if fresh else acc_in[rows, :]
        parts, weights = [], []
        for number, first, place in layout:
            parts.append(pieces[number][pl.ds(first + r * tile, tile), :])
            weights.append(w[pl.ds(pl.multiple_of(source(place) * 256, 256), 256), :])
        product = jnp.dot(
            jnp.concatenate(parts, axis=1),
            jnp.concatenate(weights, axis=0),
            preferred_element_type=F32,
        )
        total = product if fresh else total + product
        if last:
            total = total + tokens[rows, :].astype(F32)
        out[rows, :] = total.astype(out.dtype)


def out_project(length, pieces, w, state, tokens=None):
    layout, flat = number(pieces)
    rows = length
    last = tokens is not None
    ins = [w] + flat + ([] if state is None else [state]) + ([tokens] if last else [])

    def kernel(*refs):
        out_kernel(layout, state is None, last, *refs)

    outs = jax.ShapeDtypeStruct((rows, 256), BF16 if last else F32)
    aliases = {1 + len(flat): 0} if (state is not None and not last) else {}
    return call(
        kernel, outs, ins, [VMEM] * len(ins), [], 12, aliases
    )


def shifted(x, dy, dz, dc):
    pairs = []
    for i in range(16):
        y, z, c = i // 4, (i // 2) % 2, i % 2
        pairs.append((i, ((y + dy) % 4) * 4 + ((z + dz) % 2) * 2 + (c + dc) % 2))
    return lax.ppermute(x, "tp", pairs)


def tie(value, *others):
    return lax.optimization_barrier((value,) + others)[0]


def body(tokens, norm_gain, w_in, w_short, decay_rate, residue, w_out):
    length, chans = tokens.shape
    half = length // 2
    chunk = length // SUBS

    def other(p, *after):
        return shifted(tie(p, *after) if after else p, 0, 0, 1)

    def gather(x, start, add):
        far = shifted(x, 2, 0, 0)
        left = shifted(x, 1, 0, 0)
        right = shifted(x, -1, 0, 0)
        x_other = other(x)
        up = shifted(tie(x, x_other), 0, 1, 0)
        if start is not None:
            x_other = tie(x_other, start)
        state, mark = add([(x, 0, (0, 0, 0)), (x_other, 0, (0, 0, 1))], None)
        up, far, mark = lax.optimization_barrier((up, far, mark))
        up_left = shifted(up, 1, 0, 0)
        up_right = shifted(up, -1, 0, 0)
        up_far = shifted(far, 0, 1, 0)
        up_other, far_other = other(up, left, right), other(far, left, right)
        left_other, right_other = other(left), other(right)
        pieces = [(up, 0, (0, 1, 0)), (far, 0, (2, 0, 0)), (left, 0, (-1, 0, 0)), (right, 0, (1, 0, 0))]
        state, mark = add(pieces, state)
        up_left, up_right, up_far, mark = lax.optimization_barrier((up_left, up_right, up_far, mark))
        up_far_other, up_left_other, up_right_other = other(up_far), other(up_left), other(up_right)
        pieces = [(up_far, 0, (2, 1, 0)), (up_left, 0, (-1, 1, 0)), (up_right, 0, (1, 1, 0))]
        state, mark = add(pieces, state)
        pieces = [(up_other, 0, (0, 1, 1)), (far_other, 0, (2, 0, 1))]
        pieces += [(left_other, 0, (-1, 0, 1)), (right_other, 0, (1, 0, 1))]
        state, mark = add(pieces, state)
        pieces = [(up_far_other, 0, (2, 1, 1)), (up_left_other, 0, (-1, 1, 1))]
        return pieces + [(up_right_other, 0, (1, 1, 1))], state

    width = chans

    table = call(
        lambda *refs: table_kernel(chunk, *refs),
        jax.ShapeDtypeStruct((TABLE_ROWS, width), F32),
        [decay_rate.T, residue.T, w_short],
        [VMEM] * 3,
        [],
        4,
    )
    gain = norm_gain.reshape(16, width)
    first = w_in.transpose(1, 0, 2)
    second = w_out

    def add_in(pieces, state):
        state = project(length, pieces, gain, first, state)
        return state, state[0]

    pieces, state = gather(tokens, table, add_in)
    layout, flat = number(pieces)
    ins = [gain, first] + flat + list(state) + [table]

    def kernel(*refs):
        local_kernel(layout, chunk, *refs)

    gate, local, before, load = call(
        kernel,
        [
            jax.ShapeDtypeStruct((length, chans), F32),
            jax.ShapeDtypeStruct((length, chans), F32),
            jax.ShapeDtypeStruct((MODES * SUBS, chans), F32),
            jax.ShapeDtypeStruct((8, 80, chans), BF16),
        ],
        ins,
        [VMEM] * len(ins),
        [
            pltpu.VMEM((3 * chans // LANES, length + SUBS * PAD, LANES), F32),
            pltpu.VMEM((MODES, chans), F32),
        ],
        20,
    )
    loads = lax.all_to_all(load, "ctx", 0, 0, tiled=True)
    ins = [loads, gate, local, before, table]

    def kernel_two(*refs):
        join_kernel(chunk, *refs)

    mixed = call(
        kernel_two,
        jax.ShapeDtypeStruct((length, chans), BF16),
        ins,
        [VMEM] * len(ins),
        [
            pltpu.VMEM((chans // LANES, 9 * (64 + PAD), LANES), F32),
            pltpu.VMEM((chans // LANES, length + SUBS * PAD, LANES), F32),
            pltpu.VMEM((MODES * SUBS, chans), F32),
        ],
        12,
    )

    def add_out(pieces, state):
        state = out_project(length, pieces, second, state)
        return state, state

    pieces, state = gather(mixed, None, add_out)
    return out_project(length, pieces, second, state, tokens)


def solution(mesh):
    placed = (
        P("ctx", "tp"),
        P(),
        P(None, None, "tp"),
        P(None, None, "tp"),
        P("tp", None),
        P("tp", None),
        P(None, "tp"),
    )
    return jax.shard_map(
        body, mesh=mesh, in_specs=placed, out_specs=P("ctx", "tp"), check_vma=False
    )
```

```python
import jax
import jax.numpy as jnp
from jax import lax
from jax.experimental import pallas as pl
from jax.experimental.pallas import tpu as pltpu
from jax.sharding import PartitionSpec as P

F32 = jnp.float32
BF16 = jnp.bfloat16
MODES = 16
SPAN = 7
REACH = SPAN - 1
LANES = 128
SUBS = 8
VMEM = pl.BlockSpec(memory_space=pltpu.VMEM)
HBM = pl.BlockSpec(memory_space=pltpu.HBM)
SMEM = pl.BlockSpec(memory_space=pltpu.SMEM)
MIB = 1024 * 1024
TILE = 512
GROUP = 4
PAD = 8


def call(kernel, outs, ins, specs, scratch, limit, aliases=None):
    return pl.pallas_call(
        kernel,
        out_shape=outs,
        in_specs=specs,
        out_specs=[VMEM] * len(outs) if isinstance(outs, list) else VMEM,
        scratch_shapes=scratch,
        input_output_aliases=aliases or {},
        compiler_params=pltpu.CompilerParams(vmem_limit_bytes=limit * MIB),
        cost_estimate=pl.CostEstimate(flops=1, bytes_accessed=1, transcendentals=0),
    )(*ins)


TABLE = {}
for _name, _rows in (
    ("decay", MODES * SUBS),
    ("weight", MODES * SUBS),
    ("power", MODES * SUBS),
    ("power_less", MODES * SUBS),
    ("ahead", MODES * SUBS),
    ("taps", SPAN * 3 * SUBS),
    ("jumps", 3 * MODES),
    ("early", REACH * MODES),
    ("late", REACH * MODES),
):
    TABLE[_name] = (sum(rows for _, rows in TABLE.values()), _rows)
TABLE_ROWS = sum(rows for _, rows in TABLE.values())

def add_up(terms):
    while len(terms) > 1:
        terms = [a + b for a, b in zip(terms[::2], terms[1::2])] + terms[len(terms) & ~1 :]
    return terms[0]


def part(table, name):
    begin, rows = TABLE[name]
    return table.at[pl.ds(begin, rows)]


def source(place):
    me = lax.axis_index("tp")
    y, z, c = me // 4, (me // 2) % 2, me % 2
    dy, dz, dc = place
    return ((y + dy + 4) % 4) * 4 + ((z + dz) % 2) * 2 + (c + dc) % 2


def table_kernel(chunk, rate, residue, short, table):
    width = table.shape[1]
    length = SUBS * chunk
    sub = lax.broadcasted_iota(jnp.int32, (SUBS, width), 0)
    lag = sub.astype(F32)

    def put(name, row, value):
        at = TABLE[name][0] + row
        table[at : at + value.shape[0], :] = value

    rates = rate[...]
    for level, hop in enumerate((1, 2, 4)):
        put("jumps", level * MODES, jnp.exp(-rates * (chunk * hop)))
    for t in range(REACH):
        put("early", t * MODES, jnp.exp(-rates * (chunk - 1 - t)))
        put("late", t * MODES, jnp.exp(-rates * (length - 1 - t)))
    weights = residue[...] * jnp.sqrt(rates)
    decays = jnp.exp(-rates)
    for n in range(MODES):
        wide = jnp.broadcast_to(rates[n : n + 1, :], (SUBS, width))
        put("decay", n * SUBS, jnp.broadcast_to(decays[n : n + 1, :], (SUBS, width)))
        put("weight", n * SUBS, jnp.broadcast_to(weights[n : n + 1, :], (SUBS, width)))
        put("power", n * SUBS, jnp.exp(-wide * (lag * chunk)))
        less = jnp.exp(-wide * (jnp.maximum(lag - 1.0, 0.0) * chunk))
        put("power_less", n * SUBS, jnp.where(sub >= 1, less, 0.0))
        far = jnp.exp(-wide * (jnp.maximum(lag - 1.0, 0.0) * length))
        put("ahead", n * SUBS, jnp.where(sub >= 1, far, 0.0))
    for i in range(SPAN * 3):
        tap = short[i // 3, i % 3 : i % 3 + 1, :]
        put("taps", i * SUBS, jnp.broadcast_to(tap, (SUBS, width)))


def add_pieces(layout, gain, w, refs, r, tile):
    squares = None
    scaled = []
    blocks = []
    for number, first, place in layout:
        block = source(place)
        x = refs[number][pl.ds(first + r * tile, tile), :].astype(F32)
        scaled.append((x * gain[pl.ds(block, 1), :]).astype(BF16))
        square = x * x
        square = square[:, :LANES] + square[:, LANES:]
        squares = square if squares is None else squares + square
        blocks.append(pl.ds(pl.multiple_of(block * 256, 256), 256))
    scaled = jnp.concatenate(scaled, axis=1)
    total = []
    for s in range(3):
        weights = jnp.concatenate([w[s, rows, :] for rows in blocks], axis=0)
        total.append(jnp.dot(scaled, weights, preferred_element_type=F32))
    return total, squares


def proj_kernel(layout, fresh, gain, w, *refs):
    count = 1 + max(p[0] for p in layout)
    pieces = refs[:count]
    if fresh:
        acc, ss = refs[count:]
    else:
        acc_in, ss_in, acc, ss = refs[count:]
    tile = TILE
    for r in range(acc.shape[0] // tile):
        rows = pl.ds(r * tile, tile)
        total, squares = add_pieces(layout, gain, w, pieces, r, tile)
        for s in range(3):
            cols = slice(s * 256, (s + 1) * 256)
            acc[rows, cols] = total[s] if fresh else acc_in[rows, cols] + total[s]
        ss[rows, :] = squares if fresh else ss_in[rows, :] + squares


def number(pieces):
    layout, flat = [], []
    for array, first, place in pieces:
        known = [i for i, a in enumerate(flat) if a is array]
        if not known:
            flat.append(array)
        layout.append((known[0] if known else len(flat) - 1, first, place))
    return layout, flat


def project(length, pieces, gain, w, state):
    layout, flat = number(pieces)
    rows = length
    outs = [jax.ShapeDtypeStruct((rows, 768), F32), jax.ShapeDtypeStruct((rows, LANES), F32)]
    ins = [gain, w] + flat + (list(state) if state else [])
    specs = [VMEM] * len(ins)
    fresh = state is None

    def kernel(*refs):
        proj_kernel(layout, fresh, *refs)

    aliases = {} if fresh else {len(ins) - 2: 0, len(ins) - 1: 1}
    return call(kernel, outs, ins, specs, [], 16, aliases)


def local_kernel(layout, chunk, gain, w, *refs):
    count = 1 + max(p[0] for p in layout)
    pieces = refs[:count]
    acc, ss, table, gate, local, before, load, proj, last = refs[count:]
    taps, decay, weight, jumps = (part(table, n) for n in ("taps", "decay", "weight", "jumps"))
    tile = TILE
    width = gate.shape[1]
    rows_all = acc.shape[0]
    halves = width // LANES
    pitch = chunk + PAD
    proj[:, 0:PAD, :] = jnp.zeros((3 * halves, PAD, LANES), F32)
    for r in range(rows_all // tile):
        rows = pl.ds(r * tile, tile)
        total, squares = add_pieces(layout, gain, w, pieces, r, tile)
        mean = jnp.sum(ss[rows, :] + squares, axis=1, keepdims=True) / (16 * width)
        scale = lax.rsqrt(mean + 1e-05)
        for s in range(3):
            cols = slice(s * 256, (s + 1) * 256)
            value = (acc[rows, cols] + total[s]) * scale
            value = value.astype(BF16).astype(F32)
            for g in range(halves):
                for k in range(tile // chunk):
                    run = r * (tile // chunk) + k
                    piece = value[k * chunk : (k + 1) * chunk, g * LANES : (g + 1) * LANES]
                    proj[s * halves + g, pl.ds(run * pitch + PAD, chunk), :] = piece
                    if run + 1 < SUBS:
                        proj[s * halves + g, pl.ds((run + 1) * pitch, PAD), :] = piece[chunk - PAD :]
    head = lax.broadcasted_iota(jnp.int32, (SUBS, LANES), 0) == 0
    for g in range(width // LANES):
        lanes = slice(g * LANES, (g + 1) * LANES)

        def strided(s, t):
            return proj[s * halves + g, pl.ds(PAD + t, SUBS, stride=pitch), :]

        unroll = 8

        def steps(i, states, masked=False):
            begin = i * unroll
            short = []
            for s in range(3):
                rows = [strided(s, begin + u) for u in range(-REACH, unroll)]
                weights = [
                    taps[(j * 3 + s) * SUBS : (j * 3 + s + 1) * SUBS, lanes] for j in range(SPAN)
                ]
                short.append(
                    [
                        add_up([weights[j] * rows[REACH + u - j] for j in range(SPAN)])
                        for u in range(unroll)
                    ]
                )
            kv = [(short[1][u] * short[2][u]).astype(BF16).astype(F32) for u in range(unroll)]
            if masked:
                kv = [jnp.where(head, 0.0, v) if u < REACH else v for u, v in enumerate(kv)]
            outs = [None] * unroll
            later = []
            for first in range(0, MODES, GROUP):
                some = range(first, first + GROUP)
                decays = [decay[n * SUBS : (n + 1) * SUBS, lanes] for n in some]
                weights = [weight[n * SUBS : (n + 1) * SUBS, lanes] for n in some]
                now = [states[n] for n in some]
                for u in range(unroll):
                    now = [decays[k] * now[k] + kv[u] for k in range(GROUP)]
                    term = add_up([weights[k] * now[k] for k in range(GROUP)])
                    outs[u] = term if outs[u] is None else outs[u] + term
                later.extend(now)
            for u in range(unroll):
                place = pl.ds(pl.multiple_of((begin + u) * SUBS, SUBS), SUBS)
                gate[place, lanes] = short[0][u].astype(BF16).astype(F32)
                local[place, lanes] = outs[u]
            return later

        states = steps(0, [jnp.zeros((SUBS, LANES), F32)] * MODES, True)
        states = lax.fori_loop(1, chunk // unroll, steps, states)
        place = lax.broadcasted_iota(jnp.int32, (SUBS, LANES), 0)
        for n in range(MODES):
            at = n * SUBS
            state = states[n]
            for level, hop in enumerate((1, 2, 4)):
                moved = jnp.where(place >= hop, pltpu.roll(state, hop, 0), 0.0)
                jump = jumps[level * MODES + n : level * MODES + n + 1, lanes]
                state = state + jump * moved
            before[at : at + SUBS, lanes] = jnp.where(place >= 1, pltpu.roll(state, 1, 0), 0.0)
            last[n : n + 1, lanes] = state[SUBS - 1 : SUBS, :]
    high = last[...].astype(BF16)
    low = (last[...] - high.astype(F32)).astype(BF16)
    ends = [high, low]
    for s in range(3):
        sides = []
        for g in range(halves):
            tail = proj[s * halves + g, SUBS * pitch - PAD : SUBS * pitch, :]
            sides.append(jnp.concatenate([tail, proj[s * halves + g, PAD : 2 * PAD, :]], axis=0))
        ends.append(jnp.concatenate(sides, axis=1).astype(BF16))
    for i, value in enumerate(ends):
        for d in range(8):
            load[d, i * 16 : (i + 1) * 16, :] = value


def join_kernel(chunk, *refs):
    loads, gate, local, before, table, mixed, held, whole, start = refs
    names = ("taps", "decay", "weight", "power", "power_less", "ahead", "early", "late")
    taps, decay, weight, power, power_less, ahead, early, late = (part(table, n) for n in names)
    step_rows = 64 + PAD
    width = mixed.shape[1]
    me = lax.axis_index("ctx")
    for d in range(9):
        source = jnp.maximum(me - d, 0)
        value = None
        if d < 8:
            value = loads[source].astype(F32)
            value = jnp.concatenate([value[0:16] + value[16:32], value[32:]], axis=0)
            value = jnp.where(me >= d, value, 0.0)
        for g in range(width // LANES):
            piece = jnp.zeros((64, LANES), F32)
            if d < 8:
                piece = value[:, g * LANES : (g + 1) * LANES]
            held[g, d * step_rows : d * step_rows + 64, :] = piece
    place = lax.broadcasted_iota(jnp.int32, (SUBS, LANES), 0)
    head = place == 0
    for g in range(width // LANES):
        lanes = slice(g * LANES, (g + 1) * LANES)

        def strided(row):
            return held[g, pl.ds(row, SUBS, stride=step_rows), :]

        short = []
        for s in range(3):
            line = [strided(step_rows + 16 + s * 16 + 8 - REACH + t) for t in range(REACH)]
            line += [strided(24 + s * 16 + t) for t in range(REACH)]
            values = []
            for t in range(REACH):
                value = None
                for j in range(SPAN):
                    at = (j * 3 + s) * SUBS
                    term = taps[at : at + SUBS, lanes] * line[REACH + t - j]
                    value = term if value is None else value + term
                values.append(value)
            short.append(values)
        kv = [(short[1][t] * short[2][t]).astype(BF16).astype(F32) for t in range(REACH)]
        q = [short[0][t].astype(BF16).astype(F32) for t in range(REACH)]
        for n in range(MODES):
            at = n * SUBS
            full = strided(n)
            own = None
            for t in range(REACH):
                row = t * MODES + n
                full = full + late[row : row + 1, lanes] * kv[t]
                term = early[row : row + 1, lanes] * kv[t]
                own = term if own is None else own + term
            arrived = jnp.sum(ahead[at : at + SUBS, lanes] * full, axis=0, keepdims=True)
            state = before[at : at + SUBS, lanes] + power[at : at + SUBS, lanes] * arrived
            state = state + power_less[at : at + SUBS, lanes] * own[0:1, :]
            start[at : at + SUBS, lanes] = state * weight[at : at + SUBS, lanes]

        decays = [decay[n * SUBS : (n + 1) * SUBS, lanes] for n in range(MODES)]

        def step(t, states, extra, fixed):
            later = []
            for n in range(MODES):
                state = decays[n] * states[n]
                if extra is not None:
                    state = state + weight[n * SUBS : (n + 1) * SUBS, lanes] * extra
                later.append(state)
            out = add_up(later)
            rows = pl.ds(pl.multiple_of(t * SUBS, SUBS), SUBS)
            q_now = gate[rows, lanes]
            if fixed is not None:
                q_now = jnp.where(head, fixed, q_now)
            whole[g, pl.ds(t, SUBS, stride=chunk + PAD), :] = q_now * (out + local[rows, lanes])
            return later

        states = [start[n * SUBS : (n + 1) * SUBS, lanes] for n in range(MODES)]
        unroll = 8
        for t in range(unroll):
            first = t < REACH
            extra = jnp.where(head, kv[t], 0.0) if first else None
            states = step(t, states, extra, q[t] if first else None)

        def steps(i, states):
            for u in range(unroll):
                states = step(i * unroll + u, states, None, None)
            return states

        lax.fori_loop(1, chunk // unroll, steps, states)
    for g in range(width // LANES):
        for k in range(SUBS):
            rows = whole[g, k * (chunk + PAD) : k * (chunk + PAD) + chunk, :]
            mixed[k * chunk : (k + 1) * chunk, g * LANES : (g + 1) * LANES] = rows.astype(BF16)


def out_kernel(layout, fresh, last, w, *refs):
    count = 1 + max(p[0] for p in layout)
    pieces = refs[:count]
    rest = list(refs[count:])
    acc_in = None if fresh else rest.pop(0)
    tokens = rest.pop(0) if last else None
    out = rest.pop(0)
    tile = TILE
    for r in range(out.shape[0] // tile):
        rows = pl.ds(r * tile, tile)
        total = None if fresh else acc_in[rows, :]
        parts, weights = [], []
        for number, first, place in layout:
            parts.append(pieces[number][pl.ds(first + r * tile, tile), :])
            weights.append(w[pl.ds(pl.multiple_of(source(place) * 256, 256), 256), :])
        product = jnp.dot(
            jnp.concatenate(parts, axis=1),
            jnp.concatenate(weights, axis=0),
            preferred_element_type=F32,
        )
        total = product if fresh else total + product
        if last:
            total = total + tokens[rows, :].astype(F32)
        out[rows, :] = total.astype(out.dtype)


def out_project(length, pieces, w, state, tokens=None):
    layout, flat = number(pieces)
    rows = length
    last = tokens is not None
    ins = [w] + flat + ([] if state is None else [state]) + ([tokens] if last else [])

    def kernel(*refs):
        out_kernel(layout, state is None, last, *refs)

    outs = jax.ShapeDtypeStruct((rows, 256), BF16 if last else F32)
    aliases = {1 + len(flat): 0} if (state is not None and not last) else {}
    return call(
        kernel, outs, ins, [VMEM] * len(ins), [], 12, aliases
    )


def shifted(x, dy, dz, dc):
    pairs = []
    for i in range(16):
        y, z, c = i // 4, (i // 2) % 2, i % 2
        pairs.append((i, ((y + dy) % 4) * 4 + ((z + dz) % 2) * 2 + (c + dc) % 2))
    return lax.ppermute(x, "tp", pairs)


def tie(value, *others):
    return lax.optimization_barrier((value,) + others)[0]


def body(tokens, norm_gain, w_in, w_short, decay_rate, residue, w_out):
    length, chans = tokens.shape
    half = length // 2
    chunk = length // SUBS

    def other(p, *after):
        return shifted(tie(p, *after) if after else p, 0, 0, 1)

    def gather(x, start, add):
        up = shifted(x, 0, 1, 0)
        far = shifted(x, 2, 0, 0)
        left = shifted(x, 1, 0, 0)
        right = shifted(x, -1, 0, 0)
        x_other = other(x)
        if start is not None:
            x_other = tie(x_other, start)
        state, mark = add([(x, 0, (0, 0, 0)), (x_other, 0, (0, 0, 1))], None)
        far, mark = lax.optimization_barrier((far, mark))
        up, far = lax.optimization_barrier((up, far))
        up_left = shifted(up, 1, 0, 0)
        up_right = shifted(up, -1, 0, 0)
        up_far = shifted(far, 0, 1, 0)
        pair = jnp.concatenate([up, far], axis=0)
        sides = jnp.concatenate([left, right], axis=0)
        pair_other, sides_other = other(pair, sides), other(sides)
        pieces = [(pair, 0, (0, 1, 0)), (pair, length, (2, 0, 0))]
        pieces += [(sides, 0, (-1, 0, 0)), (sides, length, (1, 0, 0))]
        state, mark = add(pieces, state)
        others = [(pair_other, 0, (0, 1, 1)), (pair_other, length, (2, 0, 1))]
        others += [(sides_other, 0, (-1, 0, 1)), (sides_other, length, (1, 0, 1))]
        up_left, up_right, up_far, mark = lax.optimization_barrier((up_left, up_right, up_far, mark))
        up_far_other, up_left_other, up_right_other = other(up_far), other(up_left), other(up_right)
        pieces = [(up_far, 0, (2, 1, 0)), (up_left, 0, (-1, 1, 0)), (up_right, 0, (1, 1, 0))]
        state, mark = add(others + pieces, state)
        pieces = [(up_far_other, 0, (2, 1, 1)), (up_left_other, 0, (-1, 1, 1))]
        return pieces + [(up_right_other, 0, (1, 1, 1))], state

    width = chans

    table = call(
        lambda *refs: table_kernel(chunk, *refs),
        jax.ShapeDtypeStruct((TABLE_ROWS, width), F32),
        [decay_rate.T, residue.T, w_short],
        [VMEM] * 3,
        [],
        4,
    )
    gain = norm_gain.reshape(16, width)
    first = w_in.transpose(1, 0, 2)
    second = w_out

    def add_in(pieces, state):
        state = project(length, pieces, gain, first, state)
        return state, state[0]

    pieces, state = gather(tokens, table, add_in)
    layout, flat = number(pieces)
    ins = [gain, first] + flat + list(state) + [table]

    def kernel(*refs):
        local_kernel(layout, chunk, *refs)

    gate, local, before, load = call(
        kernel,
        [
            jax.ShapeDtypeStruct((length, chans), F32),
            jax.ShapeDtypeStruct((length, chans), F32),
            jax.ShapeDtypeStruct((MODES * SUBS, chans), F32),
            jax.ShapeDtypeStruct((8, 80, chans), BF16),
        ],
        ins,
        [VMEM] * len(ins),
        [
            pltpu.VMEM((3 * chans // LANES, length + SUBS * PAD, LANES), F32),
            pltpu.VMEM((MODES, chans), F32),
        ],
        20,
    )
    loads = lax.all_to_all(load, "ctx", 0, 0, tiled=True)
    ins = [loads, gate, local, before, table]

    def kernel_two(*refs):
        join_kernel(chunk, *refs)

    mixed = call(
        kernel_two,
        jax.ShapeDtypeStruct((length, chans), BF16),
        ins,
        [VMEM] * len(ins),
        [
            pltpu.VMEM((chans // LANES, 9 * (64 + PAD), LANES), F32),
            pltpu.VMEM((chans // LANES, length + SUBS * PAD, LANES), F32),
            pltpu.VMEM((MODES * SUBS, chans), F32),
        ],
        12,
    )

    def add_out(pieces, state):
        state = out_project(length, pieces, second, state)
        return state, state

    pieces, state = gather(mixed, None, add_out)
    return out_project(length, pieces, second, state, tokens)


def solution(mesh):
    placed = (
        P("ctx", "tp"),
        P(),
        P(None, None, "tp"),
        P(None, None, "tp"),
        P("tp", None),
        P("tp", None),
        P(None, "tp"),
    )
    return jax.shard_map(
        body, mesh=mesh, in_specs=placed, out_specs=P("ctx", "tp"), check_vma=False
    )
```

```python
import jax
import jax.numpy as jnp
from jax import lax
from jax.experimental import pallas as pl
from jax.experimental.pallas import tpu as pltpu
from jax.sharding import PartitionSpec as P

F32 = jnp.float32
BF16 = jnp.bfloat16
MODES = 16
SPAN = 7
REACH = SPAN - 1
LANES = 128
SUBS = 8
VMEM = pl.BlockSpec(memory_space=pltpu.VMEM)
HBM = pl.BlockSpec(memory_space=pltpu.HBM)
SMEM = pl.BlockSpec(memory_space=pltpu.SMEM)
MIB = 1024 * 1024
TILE = 512
GROUP = 4
PAD = 8


def call(kernel, outs, ins, specs, scratch, limit, aliases=None):
    return pl.pallas_call(
        kernel,
        out_shape=outs,
        in_specs=specs,
        out_specs=[VMEM] * len(outs) if isinstance(outs, list) else VMEM,
        scratch_shapes=scratch,
        input_output_aliases=aliases or {},
        compiler_params=pltpu.CompilerParams(vmem_limit_bytes=limit * MIB),
        cost_estimate=pl.CostEstimate(flops=1, bytes_accessed=1, transcendentals=0),
    )(*ins)


TABLE = {}
for _name, _rows in (
    ("decay", MODES * SUBS),
    ("weight", MODES * SUBS),
    ("power", MODES * SUBS),
    ("power_less", MODES * SUBS),
    ("ahead", MODES * SUBS),
    ("taps", SPAN * 3 * SUBS),
    ("jumps", 3 * MODES),
    ("early", REACH * MODES),
    ("late", REACH * MODES),
):
    TABLE[_name] = (sum(rows for _, rows in TABLE.values()), _rows)
TABLE_ROWS = sum(rows for _, rows in TABLE.values())

def add_up(terms):
    while len(terms) > 1:
        terms = [a + b for a, b in zip(terms[::2], terms[1::2])] + terms[len(terms) & ~1 :]
    return terms[0]


def part(table, name):
    begin, rows = TABLE[name]
    return table.at[pl.ds(begin, rows)]


def source(place):
    me = lax.axis_index("tp")
    y, z, c = me // 4, (me // 2) % 2, me % 2
    dy, dz, dc = place
    return ((y + dy + 4) % 4) * 4 + ((z + dz) % 2) * 2 + (c + dc) % 2


def table_kernel(chunk, rate, residue, short, table):
    width = table.shape[1]
    length = SUBS * chunk
    sub = lax.broadcasted_iota(jnp.int32, (SUBS, width), 0)
    lag = sub.astype(F32)

    def put(name, row, value):
        at = TABLE[name][0] + row
        table[at : at + value.shape[0], :] = value

    rates = rate[...]
    for level, hop in enumerate((1, 2, 4)):
        put("jumps", level * MODES, jnp.exp(-rates * (chunk * hop)))
    for t in range(REACH):
        put("early", t * MODES, jnp.exp(-rates * (chunk - 1 - t)))
        put("late", t * MODES, jnp.exp(-rates * (length - 1 - t)))
    weights = residue[...] * jnp.sqrt(rates)
    decays = jnp.exp(-rates)
    for n in range(MODES):
        wide = jnp.broadcast_to(rates[n : n + 1, :], (SUBS, width))
        put("decay", n * SUBS, jnp.broadcast_to(decays[n : n + 1, :], (SUBS, width)))
        put("weight", n * SUBS, jnp.broadcast_to(weights[n : n + 1, :], (SUBS, width)))
        put("power", n * SUBS, jnp.exp(-wide * (lag * chunk)))
        less = jnp.exp(-wide * (jnp.maximum(lag - 1.0, 0.0) * chunk))
        put("power_less", n * SUBS, jnp.where(sub >= 1, less, 0.0))
        far = jnp.exp(-wide * (jnp.maximum(lag - 1.0, 0.0) * length))
        put("ahead", n * SUBS, jnp.where(sub >= 1, far, 0.0))
    for i in range(SPAN * 3):
        tap = short[i // 3, i % 3 : i % 3 + 1, :]
        put("taps", i * SUBS, jnp.broadcast_to(tap, (SUBS, width)))


def add_pieces(layout, gain, w, refs, r, tile):
    squares = None
    scaled = []
    blocks = []
    for number, first, place in layout:
        block = source(place)
        x = refs[number][pl.ds(first + r * tile, tile), :].astype(F32)
        scaled.append((x * gain[pl.ds(block, 1), :]).astype(BF16))
        square = x * x
        square = square[:, :LANES] + square[:, LANES:]
        squares = square if squares is None else squares + square
        blocks.append(pl.ds(pl.multiple_of(block * 256, 256), 256))
    scaled = jnp.concatenate(scaled, axis=1)
    total = []
    for s in range(3):
        weights = jnp.concatenate([w[s, rows, :] for rows in blocks], axis=0)
        total.append(jnp.dot(scaled, weights, preferred_element_type=F32))
    return total, squares


def proj_kernel(layout, fresh, gain, w, *refs):
    count = 1 + max(p[0] for p in layout)
    pieces = refs[:count]
    if fresh:
        acc, ss = refs[count:]
    else:
        acc_in, ss_in, acc, ss = refs[count:]
    tile = TILE
    for r in range(acc.shape[0] // tile):
        rows = pl.ds(r * tile, tile)
        total, squares = add_pieces(layout, gain, w, pieces, r, tile)
        for s in range(3):
            cols = slice(s * 256, (s + 1) * 256)
            acc[rows, cols] = total[s] if fresh else acc_in[rows, cols] + total[s]
        ss[rows, :] = squares if fresh else ss_in[rows, :] + squares


def number(pieces):
    layout, flat = [], []
    for array, first, place in pieces:
        known = [i for i, a in enumerate(flat) if a is array]
        if not known:
            flat.append(array)
        layout.append((known[0] if known else len(flat) - 1, first, place))
    return layout, flat


def project(length, pieces, gain, w, state):
    layout, flat = number(pieces)
    rows = length
    outs = [jax.ShapeDtypeStruct((rows, 768), F32), jax.ShapeDtypeStruct((rows, LANES), F32)]
    ins = [gain, w] + flat + (list(state) if state else [])
    specs = [VMEM] * len(ins)
    fresh = state is None

    def kernel(*refs):
        proj_kernel(layout, fresh, *refs)

    aliases = {} if fresh else {len(ins) - 2: 0, len(ins) - 1: 1}
    return call(kernel, outs, ins, specs, [], 16, aliases)


def local_kernel(layout, chunk, gain, w, *refs):
    count = 1 + max(p[0] for p in layout)
    pieces = refs[:count]
    acc, ss, table, gate, local, before, load, proj, last = refs[count:]
    taps, decay, weight, jumps = (part(table, n) for n in ("taps", "decay", "weight", "jumps"))
    tile = TILE
    width = gate.shape[1]
    rows_all = acc.shape[0]
    halves = width // LANES
    pitch = chunk + PAD
    proj[:, 0:PAD, :] = jnp.zeros((3 * halves, PAD, LANES), F32)
    for r in range(rows_all // tile):
        rows = pl.ds(r * tile, tile)
        total, squares = add_pieces(layout, gain, w, pieces, r, tile)
        mean = jnp.sum(ss[rows, :] + squares, axis=1, keepdims=True) / (16 * width)
        scale = lax.rsqrt(mean + 1e-05)
        for s in range(3):
            cols = slice(s * 256, (s + 1) * 256)
            value = (acc[rows, cols] + total[s]) * scale
            value = value.astype(BF16).astype(F32)
            for g in range(halves):
                for k in range(tile // chunk):
                    run = r * (tile // chunk) + k
                    piece = value[k * chunk : (k + 1) * chunk, g * LANES : (g + 1) * LANES]
                    proj[s * halves + g, pl.ds(run * pitch + PAD, chunk), :] = piece
                    if run + 1 < SUBS:
                        proj[s * halves + g, pl.ds((run + 1) * pitch, PAD), :] = piece[chunk - PAD :]
    head = lax.broadcasted_iota(jnp.int32, (SUBS, LANES), 0) == 0
    for g in range(width // LANES):
        lanes = slice(g * LANES, (g + 1) * LANES)

        def strided(s, t):
            return proj[s * halves + g, pl.ds(PAD + t, SUBS, stride=pitch), :]

        unroll = 8

        def steps(i, states, masked=False):
            begin = i * unroll
            short = []
            for s in range(3):
                rows = [strided(s, begin + u) for u in range(-REACH, unroll)]
                weights = [
                    taps[(j * 3 + s) * SUBS : (j * 3 + s + 1) * SUBS, lanes] for j in range(SPAN)
                ]
                short.append(
                    [
                        add_up([weights[j] * rows[REACH + u - j] for j in range(SPAN)])
                        for u in range(unroll)
                    ]
                )
            kv = [short[1][u] * short[2][u] for u in range(unroll)]
            if masked:
                kv = [jnp.where(head, 0.0, v) if u < REACH else v for u, v in enumerate(kv)]
            outs = [None] * unroll
            later = []
            for first in range(0, MODES, GROUP):
                some = range(first, first + GROUP)
                decays = [decay[n * SUBS : (n + 1) * SUBS, lanes] for n in some]
                weights = [weight[n * SUBS : (n + 1) * SUBS, lanes] for n in some]
                now = [states[n] for n in some]
                for u in range(unroll):
                    now = [decays[k] * now[k] + kv[u] for k in range(GROUP)]
                    term = add_up([weights[k] * now[k] for k in range(GROUP)])
                    outs[u] = term if outs[u] is None else outs[u] + term
                later.extend(now)
            for u in range(unroll):
                place = pl.ds(pl.multiple_of((begin + u) * SUBS, SUBS), SUBS)
                gate[place, lanes] = short[0][u]
                local[place, lanes] = outs[u]
            return later

        states = steps(0, [jnp.zeros((SUBS, LANES), F32)] * MODES, True)
        states = lax.fori_loop(1, chunk // unroll, steps, states)
        place = lax.broadcasted_iota(jnp.int32, (SUBS, LANES), 0)
        for n in range(MODES):
            at = n * SUBS
            state = states[n]
            for level, hop in enumerate((1, 2, 4)):
                moved = jnp.where(place >= hop, pltpu.roll(state, hop, 0), 0.0)
                jump = jumps[level * MODES + n : level * MODES + n + 1, lanes]
                state = state + jump * moved
            before[at : at + SUBS, lanes] = jnp.where(place >= 1, pltpu.roll(state, 1, 0), 0.0)
            last[n : n + 1, lanes] = state[SUBS - 1 : SUBS, :]
    high = last[...].astype(BF16)
    low = (last[...] - high.astype(F32)).astype(BF16)
    ends = [high, low]
    for s in range(3):
        sides = []
        for g in range(halves):
            tail = proj[s * halves + g, SUBS * pitch - PAD : SUBS * pitch, :]
            sides.append(jnp.concatenate([tail, proj[s * halves + g, PAD : 2 * PAD, :]], axis=0))
        ends.append(jnp.concatenate(sides, axis=1).astype(BF16))
    for i, value in enumerate(ends):
        for d in range(8):
            load[d, i * 16 : (i + 1) * 16, :] = value


def join_kernel(chunk, *refs):
    loads, gate, local, before, table, mixed, held, whole, start = refs
    names = ("taps", "decay", "weight", "power", "power_less", "ahead", "early", "late")
    taps, decay, weight, power, power_less, ahead, early, late = (part(table, n) for n in names)
    step_rows = 64 + PAD
    width = mixed.shape[1]
    me = lax.axis_index("ctx")
    for d in range(9):
        source = jnp.maximum(me - d, 0)
        value = None
        if d < 8:
            value = loads[source].astype(F32)
            value = jnp.concatenate([value[0:16] + value[16:32], value[32:]], axis=0)
            value = jnp.where(me >= d, value, 0.0)
        for g in range(width // LANES):
            piece = jnp.zeros((64, LANES), F32)
            if d < 8:
                piece = value[:, g * LANES : (g + 1) * LANES]
            held[g, d * step_rows : d * step_rows + 64, :] = piece
    place = lax.broadcasted_iota(jnp.int32, (SUBS, LANES), 0)
    head = place == 0
    for g in range(width // LANES):
        lanes = slice(g * LANES, (g + 1) * LANES)

        def strided(row):
            return held[g, pl.ds(row, SUBS, stride=step_rows), :]

        short = []
        for s in range(3):
            line = [strided(step_rows + 16 + s * 16 + 8 - REACH + t) for t in range(REACH)]
            line += [strided(24 + s * 16 + t) for t in range(REACH)]
            values = []
            for t in range(REACH):
                value = None
                for j in range(SPAN):
                    at = (j * 3 + s) * SUBS
                    term = taps[at : at + SUBS, lanes] * line[REACH + t - j]
                    value = term if value is None else value + term
                values.append(value)
            short.append(values)
        kv = [short[1][t] * short[2][t] for t in range(REACH)]
        q = short[0]
        for n in range(MODES):
            at = n * SUBS
            full = strided(n)
            own = None
            for t in range(REACH):
                row = t * MODES + n
                full = full + late[row : row + 1, lanes] * kv[t]
                term = early[row : row + 1, lanes] * kv[t]
                own = term if own is None else own + term
            arrived = jnp.sum(ahead[at : at + SUBS, lanes] * full, axis=0, keepdims=True)
            state = before[at : at + SUBS, lanes] + power[at : at + SUBS, lanes] * arrived
            state = state + power_less[at : at + SUBS, lanes] * own[0:1, :]
            start[at : at + SUBS, lanes] = state * weight[at : at + SUBS, lanes]

        decays = [decay[n * SUBS : (n + 1) * SUBS, lanes] for n in range(MODES)]

        def step(t, states, extra, fixed):
            later = []
            for n in range(MODES):
                state = decays[n] * states[n]
                if extra is not None:
                    state = state + weight[n * SUBS : (n + 1) * SUBS, lanes] * extra
                later.append(state)
            out = add_up(later)
            rows = pl.ds(pl.multiple_of(t * SUBS, SUBS), SUBS)
            q_now = gate[rows, lanes]
            if fixed is not None:
                q_now = jnp.where(head, fixed, q_now)
            whole[g, pl.ds(t, SUBS, stride=chunk + PAD), :] = q_now * (out + local[rows, lanes])
            return later

        states = [start[n * SUBS : (n + 1) * SUBS, lanes] for n in range(MODES)]
        unroll = 8
        for t in range(unroll):
            first = t < REACH
            extra = jnp.where(head, kv[t], 0.0) if first else None
            states = step(t, states, extra, q[t] if first else None)

        def steps(i, states):
            for u in range(unroll):
                states = step(i * unroll + u, states, None, None)
            return states

        lax.fori_loop(1, chunk // unroll, steps, states)
    for g in range(width // LANES):
        for k in range(SUBS):
            rows = whole[g, k * (chunk + PAD) : k * (chunk + PAD) + chunk, :]
            mixed[k * chunk : (k + 1) * chunk, g * LANES : (g + 1) * LANES] = rows.astype(BF16)


def out_kernel(layout, fresh, last, w, *refs):
    count = 1 + max(p[0] for p in layout)
    pieces = refs[:count]
    rest = list(refs[count:])
    acc_in = None if fresh else rest.pop(0)
    tokens = rest.pop(0) if last else None
    out = rest.pop(0)
    tile = TILE
    for r in range(out.shape[0] // tile):
        rows = pl.ds(r * tile, tile)
        total = None if fresh else acc_in[rows, :]
        parts, weights = [], []
        for number, first, place in layout:
            parts.append(pieces[number][pl.ds(first + r * tile, tile), :])
            weights.append(w[pl.ds(pl.multiple_of(source(place) * 256, 256), 256), :])
        product = jnp.dot(
            jnp.concatenate(parts, axis=1),
            jnp.concatenate(weights, axis=0),
            preferred_element_type=F32,
        )
        total = product if fresh else total + product
        if last:
            total = total + tokens[rows, :].astype(F32)
        out[rows, :] = total.astype(out.dtype)


def out_project(length, pieces, w, state, tokens=None):
    layout, flat = number(pieces)
    rows = length
    last = tokens is not None
    ins = [w] + flat + ([] if state is None else [state]) + ([tokens] if last else [])

    def kernel(*refs):
        out_kernel(layout, state is None, last, *refs)

    outs = jax.ShapeDtypeStruct((rows, 256), BF16 if last else F32)
    aliases = {1 + len(flat): 0} if (state is not None and not last) else {}
    return call(
        kernel, outs, ins, [VMEM] * len(ins), [], 12, aliases
    )


def shifted(x, dy, dz, dc):
    pairs = []
    for i in range(16):
        y, z, c = i // 4, (i // 2) % 2, i % 2
        pairs.append((i, ((y + dy) % 4) * 4 + ((z + dz) % 2) * 2 + (c + dc) % 2))
    return lax.ppermute(x, "tp", pairs)


def tie(value, *others):
    return lax.optimization_barrier((value,) + others)[0]


def body(tokens, norm_gain, w_in, w_short, decay_rate, residue, w_out):
    length, chans = tokens.shape
    half = length // 2
    chunk = length // SUBS

    def other(p, *after):
        return shifted(tie(p, *after) if after else p, 0, 0, 1)

    def gather(x, start, add):
        up = shifted(x, 0, 1, 0)
        far = shifted(x, 2, 0, 0)
        left = shifted(x, 1, 0, 0)
        right = shifted(x, -1, 0, 0)
        x_other = other(x)
        if start is not None:
            x_other = tie(x_other, start)
        state, mark = add([(x, 0, (0, 0, 0)), (x_other, 0, (0, 0, 1))], None)
        far, mark = lax.optimization_barrier((far, mark))
        up, far = lax.optimization_barrier((up, far))
        up_left = shifted(up, 1, 0, 0)
        up_right = shifted(up, -1, 0, 0)
        up_far = shifted(far, 0, 1, 0)
        pair = jnp.concatenate([up, far], axis=0)
        sides = jnp.concatenate([left, right], axis=0)
        pair_other, sides_other = other(pair, sides), other(sides)
        pieces = [(pair, 0, (0, 1, 0)), (pair, length, (2, 0, 0))]
        pieces += [(sides, 0, (-1, 0, 0)), (sides, length, (1, 0, 0))]
        state, mark = add(pieces, state)
        others = [(pair_other, 0, (0, 1, 1)), (pair_other, length, (2, 0, 1))]
        others += [(sides_other, 0, (-1, 0, 1)), (sides_other, length, (1, 0, 1))]
        up_left, up_right, up_far, mark = lax.optimization_barrier((up_left, up_right, up_far, mark))
        up_far_other, up_left_other, up_right_other = other(up_far), other(up_left), other(up_right)
        pieces = [(up_far, 0, (2, 1, 0)), (up_left, 0, (-1, 1, 0)), (up_right, 0, (1, 1, 0))]
        state, mark = add(others + pieces, state)
        pieces = [(up_far_other, 0, (2, 1, 1)), (up_left_other, 0, (-1, 1, 1))]
        return pieces + [(up_right_other, 0, (1, 1, 1))], state

    width = chans

    table = call(
        lambda *refs: table_kernel(chunk, *refs),
        jax.ShapeDtypeStruct((TABLE_ROWS, width), F32),
        [decay_rate.T, residue.T, w_short],
        [VMEM] * 3,
        [],
        4,
    )
    gain = norm_gain.reshape(16, width)
    first = w_in.transpose(1, 0, 2)
    second = w_out

    def add_in(pieces, state):
        state = project(length, pieces, gain, first, state)
        return state, state[0]

    pieces, state = gather(tokens, table, add_in)
    layout, flat = number(pieces)
    ins = [gain, first] + flat + list(state) + [table]

    def kernel(*refs):
        local_kernel(layout, chunk, *refs)

    gate, local, before, load = call(
        kernel,
        [
            jax.ShapeDtypeStruct((length, chans), F32),
            jax.ShapeDtypeStruct((length, chans), F32),
            jax.ShapeDtypeStruct((MODES * SUBS, chans), F32),
            jax.ShapeDtypeStruct((8, 80, chans), BF16),
        ],
        ins,
        [VMEM] * len(ins),
        [
            pltpu.VMEM((3 * chans // LANES, length + SUBS * PAD, LANES), F32),
            pltpu.VMEM((MODES, chans), F32),
        ],
        20,
    )
    loads = lax.all_to_all(load, "ctx", 0, 0, tiled=True)
    ins = [loads, gate, local, before, table]

    def kernel_two(*refs):
        join_kernel(chunk, *refs)

    mixed = call(
        kernel_two,
        jax.ShapeDtypeStruct((length, chans), BF16),
        ins,
        [VMEM] * len(ins),
        [
            pltpu.VMEM((chans // LANES, 9 * (64 + PAD), LANES), F32),
            pltpu.VMEM((chans // LANES, length + SUBS * PAD, LANES), F32),
            pltpu.VMEM((MODES * SUBS, chans), F32),
        ],
        12,
    )

    def add_out(pieces, state):
        state = out_project(length, pieces, second, state)
        return state, state

    pieces, state = gather(mixed, None, add_out)
    return out_project(length, pieces, second, state, tokens)


def solution(mesh):
    placed = (
        P("ctx", "tp"),
        P(),
        P(None, None, "tp"),
        P(None, None, "tp"),
        P("tp", None),
        P("tp", None),
        P(None, "tp"),
    )
    return jax.shard_map(
        body, mesh=mesh, in_specs=placed, out_specs=P("ctx", "tp"), check_vma=False
    )
```

```python
import jax
import jax.numpy as jnp
from jax import lax
from jax.experimental import pallas as pl
from jax.experimental.pallas import tpu as pltpu
from jax.sharding import PartitionSpec as P

F32 = jnp.float32
BF16 = jnp.bfloat16
MODES = 16
SPAN = 7
REACH = SPAN - 1
LANES = 128
SUBS = 8
VMEM = pl.BlockSpec(memory_space=pltpu.VMEM)
HBM = pl.BlockSpec(memory_space=pltpu.HBM)
SMEM = pl.BlockSpec(memory_space=pltpu.SMEM)
MIB = 1024 * 1024
TILE = 512
GROUP = 4
PAD = 8


def call(kernel, outs, ins, specs, scratch, limit, aliases=None):
    return pl.pallas_call(
        kernel,
        out_shape=outs,
        in_specs=specs,
        out_specs=[VMEM] * len(outs) if isinstance(outs, list) else VMEM,
        scratch_shapes=scratch,
        input_output_aliases=aliases or {},
        compiler_params=pltpu.CompilerParams(vmem_limit_bytes=limit * MIB),
        cost_estimate=pl.CostEstimate(flops=1, bytes_accessed=1, transcendentals=0),
    )(*ins)


TABLE = {}
for _name, _rows in (
    ("decay", MODES * SUBS),
    ("weight", MODES * SUBS),
    ("power", MODES * SUBS),
    ("power_less", MODES * SUBS),
    ("ahead", MODES * SUBS),
    ("taps", SPAN * 3 * SUBS),
    ("jumps", 3 * MODES),
    ("early", REACH * MODES),
    ("late", REACH * MODES),
):
    TABLE[_name] = (sum(rows for _, rows in TABLE.values()), _rows)
TABLE_ROWS = sum(rows for _, rows in TABLE.values())

def add_up(terms):
    while len(terms) > 1:
        terms = [a + b for a, b in zip(terms[::2], terms[1::2])] + terms[len(terms) & ~1 :]
    return terms[0]


def part(table, name):
    begin, rows = TABLE[name]
    return table.at[pl.ds(begin, rows)]


def source(place):
    me = lax.axis_index("tp")
    y, z, c = me // 4, (me // 2) % 2, me % 2
    dy, dz, dc = place
    return ((y + dy + 4) % 4) * 4 + ((z + dz) % 2) * 2 + (c + dc) % 2


def table_kernel(chunk, rate, residue, short, table):
    width = table.shape[1]
    length = SUBS * chunk
    sub = lax.broadcasted_iota(jnp.int32, (SUBS, width), 0)
    lag = sub.astype(F32)

    def put(name, row, value):
        at = TABLE[name][0] + row
        table[at : at + value.shape[0], :] = value

    rates = rate[...]
    for level, hop in enumerate((1, 2, 4)):
        put("jumps", level * MODES, jnp.exp(-rates * (chunk * hop)))
    for t in range(REACH):
        put("early", t * MODES, jnp.exp(-rates * (chunk - 1 - t)))
        put("late", t * MODES, jnp.exp(-rates * (length - 1 - t)))
    weights = residue[...] * jnp.sqrt(rates)
    decays = jnp.exp(-rates)
    for n in range(MODES):
        wide = jnp.broadcast_to(rates[n : n + 1, :], (SUBS, width))
        put("decay", n * SUBS, jnp.broadcast_to(decays[n : n + 1, :], (SUBS, width)))
        put("weight", n * SUBS, jnp.broadcast_to(weights[n : n + 1, :], (SUBS, width)))
        put("power", n * SUBS, jnp.exp(-wide * (lag * chunk)))
        less = jnp.exp(-wide * (jnp.maximum(lag - 1.0, 0.0) * chunk))
        put("power_less", n * SUBS, jnp.where(sub >= 1, less, 0.0))
        far = jnp.exp(-wide * (jnp.maximum(lag - 1.0, 0.0) * length))
        put("ahead", n * SUBS, jnp.where(sub >= 1, far, 0.0))
    for i in range(SPAN * 3):
        tap = short[i // 3, i % 3 : i % 3 + 1, :]
        put("taps", i * SUBS, jnp.broadcast_to(tap, (SUBS, width)))


def add_pieces(layout, gain, w, refs, r, tile):
    squares = None
    scaled = []
    blocks = []
    for number, first, place in layout:
        block = source(place)
        x = refs[number][pl.ds(first + r * tile, tile), :].astype(F32)
        scaled.append((x * gain[pl.ds(block, 1), :]).astype(BF16))
        square = x * x
        square = square[:, :LANES] + square[:, LANES:]
        squares = square if squares is None else squares + square
        blocks.append(pl.ds(pl.multiple_of(block * 256, 256), 256))
    scaled = jnp.concatenate(scaled, axis=1)
    total = []
    for s in range(3):
        weights = jnp.concatenate([w[s, rows, :] for rows in blocks], axis=0)
        total.append(jnp.dot(scaled, weights, preferred_element_type=F32))
    return total, squares


def proj_kernel(layout, fresh, gain, w, *refs):
    count = 1 + max(p[0] for p in layout)
    pieces = refs[:count]
    if fresh:
        acc, ss = refs[count:]
    else:
        acc_in, ss_in, acc, ss = refs[count:]
    tile = TILE
    for r in range(acc.shape[0] // tile):
        rows = pl.ds(r * tile, tile)
        total, squares = add_pieces(layout, gain, w, pieces, r, tile)
        for s in range(3):
            cols = slice(s * 256, (s + 1) * 256)
            acc[rows, cols] = total[s] if fresh else acc_in[rows, cols] + total[s]
        ss[rows, :] = squares if fresh else ss_in[rows, :] + squares


def number(pieces):
    layout, flat = [], []
    for array, first, place in pieces:
        known = [i for i, a in enumerate(flat) if a is array]
        if not known:
            flat.append(array)
        layout.append((known[0] if known else len(flat) - 1, first, place))
    return layout, flat


def project(length, pieces, gain, w, state):
    layout, flat = number(pieces)
    rows = length
    outs = [jax.ShapeDtypeStruct((rows, 768), F32), jax.ShapeDtypeStruct((rows, LANES), F32)]
    ins = [gain, w] + flat + (list(state) if state else [])
    specs = [VMEM] * len(ins)
    fresh = state is None

    def kernel(*refs):
        proj_kernel(layout, fresh, *refs)

    aliases = {} if fresh else {len(ins) - 2: 0, len(ins) - 1: 1}
    return call(kernel, outs, ins, specs, [], 16, aliases)


def local_kernel(layout, chunk, gain, w, *refs):
    count = 1 + max(p[0] for p in layout)
    pieces = refs[:count]
    acc, ss, table, gate, local, before, load, proj, last = refs[count:]
    taps, decay, weight, jumps = (part(table, n) for n in ("taps", "decay", "weight", "jumps"))
    tile = TILE
    width = gate.shape[1]
    rows_all = acc.shape[0]
    halves = width // LANES
    pitch = chunk + PAD
    proj[:, 0:PAD, :] = jnp.zeros((3 * halves, PAD, LANES), F32)
    for r in range(rows_all // tile):
        rows = pl.ds(r * tile, tile)
        total, squares = add_pieces(layout, gain, w, pieces, r, tile)
        mean = jnp.sum(ss[rows, :] + squares, axis=1, keepdims=True) / (16 * width)
        scale = lax.rsqrt(mean + 1e-05)
        for s in range(3):
            cols = slice(s * 256, (s + 1) * 256)
            value = (acc[rows, cols] + total[s]) * scale
            value = value.astype(BF16).astype(F32)
            for g in range(halves):
                for k in range(tile // chunk):
                    run = r * (tile // chunk) + k
                    piece = value[k * chunk : (k + 1) * chunk, g * LANES : (g + 1) * LANES]
                    proj[s * halves + g, pl.ds(run * pitch + PAD, chunk), :] = piece
                    if run + 1 < SUBS:
                        proj[s * halves + g, pl.ds((run + 1) * pitch, PAD), :] = piece[chunk - PAD :]
    head = lax.broadcasted_iota(jnp.int32, (SUBS, LANES), 0) == 0
    for g in range(width // LANES):
        lanes = slice(g * LANES, (g + 1) * LANES)

        def strided(s, t):
            return proj[s * halves + g, pl.ds(PAD + t, SUBS, stride=pitch), :]

        unroll = 16

        def steps(i, states, masked=False):
            begin = i * unroll
            short = []
            for s in range(3):
                rows = [strided(s, begin + u) for u in range(-REACH, unroll)]
                weights = [
                    taps[(j * 3 + s) * SUBS : (j * 3 + s + 1) * SUBS, lanes] for j in range(SPAN)
                ]
                short.append(
                    [
                        add_up([weights[j] * rows[REACH + u - j] for j in range(SPAN)])
                        for u in range(unroll)
                    ]
                )
            kv = [short[1][u] * short[2][u] for u in range(unroll)]
            if masked:
                kv = [jnp.where(head, 0.0, v) if u < REACH else v for u, v in enumerate(kv)]
            for u in range(unroll):
                place = pl.ds(pl.multiple_of((begin + u) * SUBS, SUBS), SUBS)
                gate[place, lanes] = short[0][u]
            outs = [None] * unroll
            later = []
            for first in range(0, MODES, GROUP):
                some = range(first, first + GROUP)
                decays = [decay[n * SUBS : (n + 1) * SUBS, lanes] for n in some]
                weights = [weight[n * SUBS : (n + 1) * SUBS, lanes] for n in some]
                now = [states[n] for n in some]
                for u in range(unroll):
                    now = [decays[k] * now[k] + kv[u] for k in range(GROUP)]
                    term = add_up([weights[k] * now[k] for k in range(GROUP)])
                    outs[u] = term if outs[u] is None else outs[u] + term
                later.extend(now)
            for u in range(unroll):
                place = pl.ds(pl.multiple_of((begin + u) * SUBS, SUBS), SUBS)
                local[place, lanes] = outs[u]
            return later

        states = steps(0, [jnp.zeros((SUBS, LANES), F32)] * MODES, True)
        states = lax.fori_loop(1, chunk // unroll, steps, states)
        place = lax.broadcasted_iota(jnp.int32, (SUBS, LANES), 0)
        for n in range(MODES):
            at = n * SUBS
            state = states[n]
            for level, hop in enumerate((1, 2, 4)):
                moved = jnp.where(place >= hop, pltpu.roll(state, hop, 0), 0.0)
                jump = jumps[level * MODES + n : level * MODES + n + 1, lanes]
                state = state + jump * moved
            before[at : at + SUBS, lanes] = jnp.where(place >= 1, pltpu.roll(state, 1, 0), 0.0)
            last[n : n + 1, lanes] = state[SUBS - 1 : SUBS, :]
    high = last[...].astype(BF16)
    low = (last[...] - high.astype(F32)).astype(BF16)
    ends = [high, low]
    for s in range(3):
        sides = []
        for g in range(halves):
            tail = proj[s * halves + g, SUBS * pitch - PAD : SUBS * pitch, :]
            sides.append(jnp.concatenate([tail, proj[s * halves + g, PAD : 2 * PAD, :]], axis=0))
        ends.append(jnp.concatenate(sides, axis=1).astype(BF16))
    for i, value in enumerate(ends):
        for d in range(8):
            load[d, i * 16 : (i + 1) * 16, :] = value


def join_kernel(chunk, *refs):
    loads, gate, local, before, table, mixed, held, whole, start = refs
    names = ("taps", "decay", "weight", "power", "power_less", "ahead", "early", "late")
    taps, decay, weight, power, power_less, ahead, early, late = (part(table, n) for n in names)
    step_rows = 64 + PAD
    width = mixed.shape[1]
    me = lax.axis_index("ctx")
    for d in range(9):
        source = jnp.maximum(me - d, 0)
        value = None
        if d < 8:
            value = loads[source].astype(F32)
            value = jnp.concatenate([value[0:16] + value[16:32], value[32:]], axis=0)
            value = jnp.where(me >= d, value, 0.0)
        for g in range(width // LANES):
            piece = jnp.zeros((64, LANES), F32)
            if d < 8:
                piece = value[:, g * LANES : (g + 1) * LANES]
            held[g, d * step_rows : d * step_rows + 64, :] = piece
    place = lax.broadcasted_iota(jnp.int32, (SUBS, LANES), 0)
    head = place == 0
    for g in range(width // LANES):
        lanes = slice(g * LANES, (g + 1) * LANES)

        def strided(row):
            return held[g, pl.ds(row, SUBS, stride=step_rows), :]

        short = []
        for s in range(3):
            line = [strided(step_rows + 16 + s * 16 + 8 - REACH + t) for t in range(REACH)]
            line += [strided(24 + s * 16 + t) for t in range(REACH)]
            values = []
            for t in range(REACH):
                value = None
                for j in range(SPAN):
                    at = (j * 3 + s) * SUBS
                    term = taps[at : at + SUBS, lanes] * line[REACH + t - j]
                    value = term if value is None else value + term
                values.append(value)
            short.append(values)
        kv = [short[1][t] * short[2][t] for t in range(REACH)]
        q = short[0]
        for n in range(MODES):
            at = n * SUBS
            full = strided(n)
            own = None
            for t in range(REACH):
                row = t * MODES + n
                full = full + late[row : row + 1, lanes] * kv[t]
                term = early[row : row + 1, lanes] * kv[t]
                own = term if own is None else own + term
            arrived = jnp.sum(ahead[at : at + SUBS, lanes] * full, axis=0, keepdims=True)
            state = before[at : at + SUBS, lanes] + power[at : at + SUBS, lanes] * arrived
            state = state + power_less[at : at + SUBS, lanes] * own[0:1, :]
            start[at : at + SUBS, lanes] = state * weight[at : at + SUBS, lanes]

        decays = [decay[n * SUBS : (n + 1) * SUBS, lanes] for n in range(MODES)]

        def step(t, states, extra, fixed):
            later = []
            for n in range(MODES):
                state = decays[n] * states[n]
                if extra is not None:
                    state = state + weight[n * SUBS : (n + 1) * SUBS, lanes] * extra
                later.append(state)
            out = add_up(later)
            rows = pl.ds(pl.multiple_of(t * SUBS, SUBS), SUBS)
            q_now = gate[rows, lanes]
            if fixed is not None:
                q_now = jnp.where(head, fixed, q_now)
            whole[g, pl.ds(t, SUBS, stride=chunk + PAD), :] = q_now * (out + local[rows, lanes])
            return later

        states = [start[n * SUBS : (n + 1) * SUBS, lanes] for n in range(MODES)]
        unroll = 8
        for t in range(unroll):
            first = t < REACH
            extra = jnp.where(head, kv[t], 0.0) if first else None
            states = step(t, states, extra, q[t] if first else None)

        def steps(i, states):
            for u in range(unroll):
                states = step(i * unroll + u, states, None, None)
            return states

        lax.fori_loop(1, chunk // unroll, steps, states)
    for g in range(width // LANES):
        for k in range(SUBS):
            rows = whole[g, k * (chunk + PAD) : k * (chunk + PAD) + chunk, :]
            mixed[k * chunk : (k + 1) * chunk, g * LANES : (g + 1) * LANES] = rows.astype(BF16)


def out_kernel(layout, fresh, last, w, *refs):
    count = 1 + max(p[0] for p in layout)
    pieces = refs[:count]
    rest = list(refs[count:])
    acc_in = None if fresh else rest.pop(0)
    tokens = rest.pop(0) if last else None
    out = rest.pop(0)
    tile = TILE
    for r in range(out.shape[0] // tile):
        rows = pl.ds(r * tile, tile)
        total = None if fresh else acc_in[rows, :]
        parts, weights = [], []
        for number, first, place in layout:
            parts.append(pieces[number][pl.ds(first + r * tile, tile), :])
            weights.append(w[pl.ds(pl.multiple_of(source(place) * 256, 256), 256), :])
        product = jnp.dot(
            jnp.concatenate(parts, axis=1),
            jnp.concatenate(weights, axis=0),
            preferred_element_type=F32,
        )
        total = product if fresh else total + product
        if last:
            total = total + tokens[rows, :].astype(F32)
        out[rows, :] = total.astype(out.dtype)


def out_project(length, pieces, w, state, tokens=None):
    layout, flat = number(pieces)
    rows = length
    last = tokens is not None
    ins = [w] + flat + ([] if state is None else [state]) + ([tokens] if last else [])

    def kernel(*refs):
        out_kernel(layout, state is None, last, *refs)

    outs = jax.ShapeDtypeStruct((rows, 256), BF16 if last else F32)
    aliases = {1 + len(flat): 0} if (state is not None and not last) else {}
    return call(
        kernel, outs, ins, [VMEM] * len(ins), [], 12, aliases
    )


def shifted(x, dy, dz, dc):
    pairs = []
    for i in range(16):
        y, z, c = i // 4, (i // 2) % 2, i % 2
        pairs.append((i, ((y + dy) % 4) * 4 + ((z + dz) % 2) * 2 + (c + dc) % 2))
    return lax.ppermute(x, "tp", pairs)


def tie(value, *others):
    return lax.optimization_barrier((value,) + others)[0]


def body(tokens, norm_gain, w_in, w_short, decay_rate, residue, w_out):
    length, chans = tokens.shape
    half = length // 2
    chunk = length // SUBS

    def other(p, *after):
        return shifted(tie(p, *after) if after else p, 0, 0, 1)

    def gather(x, start, add):
        up = shifted(x, 0, 1, 0)
        far = shifted(x, 2, 0, 0)
        left = shifted(x, 1, 0, 0)
        right = shifted(x, -1, 0, 0)
        x_other = other(x)
        if start is not None:
            x_other = tie(x_other, start)
        state, mark = add([(x, 0, (0, 0, 0)), (x_other, 0, (0, 0, 1))], None)
        far, mark = lax.optimization_barrier((far, mark))
        up, far = lax.optimization_barrier((up, far))
        up_left = shifted(up, 1, 0, 0)
        up_right = shifted(up, -1, 0, 0)
        up_far = shifted(far, 0, 1, 0)
        pair = jnp.concatenate([up, far], axis=0)
        sides = jnp.concatenate([left, right], axis=0)
        pair_other, sides_other = other(pair, sides), other(sides)
        pieces = [(pair, 0, (0, 1, 0)), (pair, length, (2, 0, 0))]
        pieces += [(sides, 0, (-1, 0, 0)), (sides, length, (1, 0, 0))]
        state, mark = add(pieces, state)
        others = [(pair_other, 0, (0, 1, 1)), (pair_other, length, (2, 0, 1))]
        others += [(sides_other, 0, (-1, 0, 1)), (sides_other, length, (1, 0, 1))]
        up_left, up_right, up_far, mark = lax.optimization_barrier((up_left, up_right, up_far, mark))
        up_far_other, up_left_other, up_right_other = other(up_far), other(up_left), other(up_right)
        pieces = [(up_far, 0, (2, 1, 0)), (up_left, 0, (-1, 1, 0)), (up_right, 0, (1, 1, 0))]
        state, mark = add(others + pieces, state)
        pieces = [(up_far_other, 0, (2, 1, 1)), (up_left_other, 0, (-1, 1, 1))]
        return pieces + [(up_right_other, 0, (1, 1, 1))], state

    width = chans

    table = call(
        lambda *refs: table_kernel(chunk, *refs),
        jax.ShapeDtypeStruct((TABLE_ROWS, width), F32),
        [decay_rate.T, residue.T, w_short],
        [VMEM] * 3,
        [],
        4,
    )
    gain = norm_gain.reshape(16, width)
    first = w_in.transpose(1, 0, 2)
    second = w_out

    def add_in(pieces, state):
        state = project(length, pieces, gain, first, state)
        return state, state[0]

    pieces, state = gather(tokens, table, add_in)
    layout, flat = number(pieces)
    ins = [gain, first] + flat + list(state) + [table]

    def kernel(*refs):
        local_kernel(layout, chunk, *refs)

    gate, local, before, load = call(
        kernel,
        [
            jax.ShapeDtypeStruct((length, chans), F32),
            jax.ShapeDtypeStruct((length, chans), F32),
            jax.ShapeDtypeStruct((MODES * SUBS, chans), F32),
            jax.ShapeDtypeStruct((8, 80, chans), BF16),
        ],
        ins,
        [VMEM] * len(ins),
        [
            pltpu.VMEM((3 * chans // LANES, length + SUBS * PAD, LANES), F32),
            pltpu.VMEM((MODES, chans), F32),
        ],
        20,
    )
    loads = lax.all_to_all(load, "ctx", 0, 0, tiled=True)
    ins = [loads, gate, local, before, table]

    def kernel_two(*refs):
        join_kernel(chunk, *refs)

    mixed = call(
        kernel_two,
        jax.ShapeDtypeStruct((length, chans), BF16),
        ins,
        [VMEM] * len(ins),
        [
            pltpu.VMEM((chans // LANES, 9 * (64 + PAD), LANES), F32),
            pltpu.VMEM((chans // LANES, length + SUBS * PAD, LANES), F32),
            pltpu.VMEM((MODES * SUBS, chans), F32),
        ],
        12,
    )

    def add_out(pieces, state):
        state = out_project(length, pieces, second, state)
        return state, state

    pieces, state = gather(mixed, None, add_out)
    return out_project(length, pieces, second, state, tokens)


def solution(mesh):
    placed = (
        P("ctx", "tp"),
        P(),
        P(None, None, "tp"),
        P(None, None, "tp"),
        P("tp", None),
        P("tp", None),
        P(None, "tp"),
    )
    return jax.shard_map(
        body, mesh=mesh, in_specs=placed, out_specs=P("ctx", "tp"), check_vma=False
    )
```
